32 devices in a mesh: dom: 16 (over z, y, x), cls: 2 (over core).
Axes of the slice: x: 2, y: 2, z: 4, core: 2. Of those that a mesh axis runs over, the one named last changes fastest.
Arguments:
- particles: bfloat16 [2048, 4608], P('dom'), may hold values from -80 to 80
- references: bfloat16 [32, 4608], P(('cls', 'dom')), may hold values from -0.77 to 0.77
- log_prior: float32 [32], P('cls'), may hold values from -3 to 3
- noise_var: float32 [32], replicated, may hold values from 0.5 to 2
- offsets: int32 [2048, 2], P('dom'), may hold values from -4 to 4
- groups: int32 [2048], P('dom'), may hold values from 0 to 15
Outputs:
- class_data: float32 [32, 4608], P(('cls', 'dom'))
- class_weight: float32 [32, 32], P(('cls', 'dom'))
- log_evidence: float32 [2048], P('dom')
The draws below stay inside these ranges and needn't reach their ends.
All inputs are finite; a program needn't handle non-finite values.
Results may differ from the reference program's by a relative error of at most 0.011.
Values may be sent and summed in bfloat16 or wider, within the bound.
No kernel may reach another device: no remote copies, remote signals or barrier semaphores. Data moves between devices by JAX's collectives and lax.ppermute only.
A program may use at most 64 MiB of HBM per device.

```python
import math
import jax
import jax.numpy as jnp
from jax import lax

BOX = 64
CYCLES = 32
ROT = 36
ANGLES = 72
SAMPLES = 4608
GROUPS = 16
PART = 2048
KLASS = 32


def shared_offsets(key):
    return jax.random.randint(jax.random.fold_in(key, 101), (PART, 2), -4, 5, dtype=jnp.int32)


def shared_groups(key):
    return jax.random.randint(jax.random.fold_in(key, 102), (PART,), 0, GROUPS, dtype=jnp.int32)


def shared_noise(key):
    return jnp.exp(jax.random.uniform(jax.random.fold_in(key, 103), (CYCLES,), jnp.float32, math.log(0.5), math.log(2.0)))


def shared_refs(key):
    values = jax.random.normal(jax.random.fold_in(key, 104), (KLASS, SAMPLES), jnp.float32)
    return 0.19 * jnp.clip(values, -4.0, 4.0)


def phase_table(offsets, groups):
    radius = jnp.arange(CYCLES, dtype=jnp.float32) + 1.0
    angle_rad = 2.0 * math.pi * jnp.arange(ANGLES, dtype=jnp.float32) / ANGLES
    shift_x = offsets[:, 0].astype(jnp.float32)
    shift_y = offsets[:, 1].astype(jnp.float32)
    phase_angle = -2.0 * math.pi / BOX * radius[None, None, :] * (shift_x[:, None, None] * jnp.cos(angle_rad)[None, :, None] + shift_y[:, None, None] * jnp.sin(angle_rad)[None, :, None])
    frequency = radius / (1.5 * BOX)
    defocus = 10000.0 + 1500.0 * groups.astype(jnp.float32)
    chi_value = math.pi * 0.0197 * defocus[:, None] * (frequency * frequency)[None, :]
    ctf_rows = -(0.995 * jnp.sin(chi_value) + 0.1 * jnp.cos(chi_value)) * jnp.exp(-10.0 * frequency * frequency)[None, :]
    return (ctf_rows, jnp.cos(phase_angle), jnp.sin(phase_angle))


def drawn_rows(key):
    ref_table = shared_refs(key)
    sample_index = jnp.arange(SAMPLES, dtype=jnp.int32)
    shift_unit = SAMPLES // ROT
    first_class = jax.random.randint(jax.random.fold_in(key, 107), (PART,), 0, KLASS, dtype=jnp.int32)
    first_rot = jax.random.randint(jax.random.fold_in(key, 108), (PART,), 0, ROT, dtype=jnp.int32)
    second_rot = (first_rot + jax.random.randint(jax.random.fold_in(key, 109), (PART,), 1, ROT, dtype=jnp.int32)) % ROT
    first_view = ref_table[first_class[:, None], (sample_index[None, :] - first_rot[:, None] * shift_unit) % SAMPLES]
    second_view = ref_table[first_class[:, None], (sample_index[None, :] - second_rot[:, None] * shift_unit) % SAMPLES]
    ctf_rows, cosine, sine_part = phase_table(shared_offsets(key), shared_groups(key))
    cycle_power = ctf_rows * ctf_rows / shared_noise(key)[None, :]
    sample_power = jnp.broadcast_to(cycle_power[:, None, None, :], (PART, ANGLES, 2, CYCLES)).reshape(PART, SAMPLES)
    energy = jnp.sum(sample_power * first_view * first_view, axis=1)
    intersection = jnp.sum(sample_power * first_view * second_view, axis=1)
    target = 150.0 + 100.0 * (jnp.arange(PART, dtype=jnp.int32) // 32 % 3).astype(jnp.float32)
    strength = target / energy
    score_gap = jax.random.uniform(jax.random.fold_in(key, 110), (PART,), jnp.float32, 1.0, 3.0)
    second_strength = strength - score_gap / (energy - intersection)
    model = (strength[:, None] * first_view + second_strength[:, None] * second_view).reshape(PART, ANGLES, 2, CYCLES)
    real_part = model[:, :, 0, :]
    imag_part = model[:, :, 1, :]
    real_obs = ctf_rows[:, None, :] * (real_part * cosine - imag_part * sine_part)
    imag_obs = ctf_rows[:, None, :] * (real_part * sine_part + imag_part * cosine)
    return jnp.stack([real_obs, imag_obs], axis=2).reshape(PART, SAMPLES)


def draw_offsets(key, part):
    return shared_offsets(key)


def draw_groups(key, part):
    return shared_groups(key)


def draw_noise_var(key, part):
    return shared_noise(key)


def draw_references(key, part):
    return shared_refs(key).astype(jnp.bfloat16)


def draw_particles(key, part):
    noise_field = jnp.clip(jax.random.normal(jax.random.fold_in(key, 105), (PART, SAMPLES), jnp.float32), -8.0, 8.0)
    chosen = jnp.arange(PART, dtype=jnp.int32) % 32 == 0
    noise_field = jnp.where(chosen[:, None], drawn_rows(key), noise_field)
    return jnp.clip(noise_field, -80.0, 80.0).astype(jnp.bfloat16)


def shard_levels(own_key, dims, shards, low, top_value):
    loudness, own = 1.0, jax.random.fold_in(own_key, 6)
    for axis_at, shards_of in shards:
        heights = jnp.exp(jax.random.uniform(jax.random.fold_in(own, axis_at), (shards_of,), jnp.float32, low / len(shards), top_value / len(shards)))
        loudness = loudness * jnp.repeat(heights, dims[axis_at] // shards_of).reshape([-1 if axis == axis_at else 1 for axis in range(len(dims))])
    return loudness


def centred(rng, extent, deviation, limit, shards=(), held_as=jnp.bfloat16):
    gain = shard_levels(rng, extent, shards, -0.22, 0.18) if shards else 1.0
    drawn = jax.random.normal(rng, extent, jnp.float32) * deviation * gain
    return jnp.minimum(jnp.maximum(drawn, -limit), limit).astype(held_as)


def setup_inputs(seed: int = 0) -> dict:
    splits = jax.random.split(jax.random.key(seed), 7)
    particles = draw_particles(jax.random.fold_in(splits[6], 71), 0)
    references = draw_references(jax.random.fold_in(splits[6], 71), 0)
    log_prior = centred(splits[2], (KLASS,), 1.0, 3.0, ((0, 2),), jnp.float32)
    noise_var = draw_noise_var(jax.random.fold_in(splits[6], 71), 0)
    offsets = draw_offsets(jax.random.fold_in(splits[6], 71), 0)
    groups = draw_groups(jax.random.fold_in(splits[6], 71), 0)
    return {"particles": particles, "references": references, "log_prior": log_prior, "noise_var": noise_var, "offsets": offsets, "groups": groups}


def prepare(observed_raw, offsets, groups, noise_var):
    row_count = observed_raw.shape[0]
    observed = observed_raw.astype(jnp.float32).reshape(row_count, ANGLES, 2, CYCLES)
    radius = jnp.arange(CYCLES, dtype=jnp.float32) + 1.0
    angle_rad = 2.0 * math.pi * jnp.arange(ANGLES, dtype=jnp.float32) / ANGLES
    shift_x = offsets[:, 0].astype(jnp.float32)
    shift_y = offsets[:, 1].astype(jnp.float32)
    phase_angle = (-2.0 * math.pi / BOX) * radius[None, None, :] * (
        shift_x[:, None, None] * jnp.cos(angle_rad)[None, :, None]
        + shift_y[:, None, None] * jnp.sin(angle_rad)[None, :, None])
    frequency = radius / (1.5 * BOX)
    defocus = 10000.0 + 1500.0 * groups.astype(jnp.float32)
    chi_value = math.pi * 0.0197 * defocus[:, None] * (frequency * frequency)[None, :]
    ctf_rows = -(0.995 * jnp.sin(chi_value) + 0.1 * jnp.cos(chi_value)) * jnp.exp(-10.0 * frequency * frequency)[None, :]
    cycle_scale = ctf_rows / noise_var[None, :]
    cosine = jnp.cos(phase_angle)
    sine_part = jnp.sin(phase_angle)
    real_in = observed[:, :, 0, :]
    imag_in = observed[:, :, 1, :]
    real_out = cycle_scale[:, None, :] * (real_in * cosine + imag_in * sine_part)
    imag_out = cycle_scale[:, None, :] * (imag_in * cosine - real_in * sine_part)
    adjusted = jnp.stack([real_out, imag_out], axis=2).reshape(row_count, SAMPLES).astype(jnp.bfloat16)
    ctf_power = ctf_rows * ctf_rows / noise_var[None, :]
    return adjusted, ctf_power


def reference(particles, references, log_prior, noise_var, offsets, groups):
    block_rows = math.gcd(PART, 512)
    block_count = PART // block_rows
    shift_unit = SAMPLES // ROT
    ref_float = references.astype(jnp.float32).reshape(KLASS, 2 * ANGLES, CYCLES)
    ref_power = jnp.sum(ref_float * ref_float, axis=1)
    ref_turned = references.T

    def one_block(carry, block_idx):
        class_data, class_weight = carry
        start = (block_idx * block_rows).astype(jnp.int32)
        part_rows = lax.dynamic_slice_in_dim(particles, start, block_rows, 0)
        offset_rows = lax.dynamic_slice_in_dim(offsets, start, block_rows, 0)
        group_rows = lax.dynamic_slice_in_dim(groups, start, block_rows, 0)
        adjusted, ctf_power = prepare(part_rows, offset_rows, group_rows, noise_var)
        doubled = jnp.concatenate([adjusted, adjusted], axis=1)
        cross_terms = jnp.stack([
            jnp.dot(doubled[:, rot_idx * shift_unit: rot_idx * shift_unit + SAMPLES], ref_turned,
                    preferred_element_type=jnp.float32)
            for rot_idx in range(ROT)])
        energy = 0.5 * jnp.dot(ctf_power, ref_power.T, precision=lax.Precision.HIGHEST)
        scores = cross_terms - energy[None, :, :] + log_prior[None, None, :]
        best = jnp.max(scores, axis=(0, 2))
        total_sum = jnp.sum(jnp.exp(scores - best[None, :, None]), axis=(0, 2))
        log_evidence = best + jnp.log(total_sum)
        posterior = jnp.exp(scores - log_evidence[None, :, None])
        posterior_bf = posterior.astype(jnp.bfloat16)
        for rot_idx in range(ROT):
            rotated = doubled[:, rot_idx * shift_unit: rot_idx * shift_unit + SAMPLES]
            class_data = class_data + jnp.dot(posterior_bf[rot_idx].T, rotated, preferred_element_type=jnp.float32)
        class_weight = class_weight + jnp.dot(jnp.sum(posterior, axis=0).T, ctf_power,
                                              precision=lax.Precision.HIGHEST)
        return (class_data, class_weight), log_evidence

    start_carry = (jnp.zeros((KLASS, SAMPLES), jnp.float32), jnp.zeros((KLASS, CYCLES), jnp.float32))
    (class_data, class_weight), evidence_rows = lax.scan(one_block, start_carry,
                                                         jnp.arange(block_count, dtype=jnp.int32))
    return class_data, class_weight, evidence_rows.reshape(PART)
```

```python
import functools
import math

import jax
import jax.numpy as jnp
import numpy as np
from jax import lax
from jax.experimental import pallas as pl
from jax.experimental.pallas import tpu as pltpu
from jax.sharding import PartitionSpec as P

BOX = 64
CYCLES = 32
ROT = 36
ANGLES = 72
LANES = 128
HALF = ROT // 2
CHUNK = 40
F32 = jnp.float32
BF16 = jnp.bfloat16
HIGHEST = lax.Precision.HIGHEST
VMEM_LIMIT = 24 * 1024 * 1024


def trig_polynomials():
    nodes = 0.125 + 0.125 * np.cos(np.pi * (np.arange(400) + 0.5) / 400)
    root = np.sqrt(nodes)
    fits = []
    for values, degree in ((np.cos(2 * np.pi * root), 7), (np.sin(2 * np.pi * root) / root, 7)):
        fit = np.polynomial.Chebyshev.fit(nodes, values, degree, domain=[0, 0.25])
        fits.append([float(c) for c in fit.convert(kind=np.polynomial.Polynomial).coef])
    return fits


COS_COEF, SIN_COEF = trig_polynomials()


def horner(coef, x):
    total = coef[-1] * x + coef[-2]
    for c in coef[-3::-1]:
        total = total * x + c
    return total


def turn_trig(turns):
    r = turns - jnp.floor(turns + 0.5)
    square = r * r
    return horner(COS_COEF, square), horner(SIN_COEF, square) * r


def lane_tables():
    lane = np.arange(LANES)
    cycle = lane % CYCLES
    rows = []
    for component in (np.cos, np.sin):
        for t in range(HALF):
            theta = 2.0 * np.pi * (2 * t + lane // 64) / ANGLES
            rows.append((cycle + 1.0) * component(theta) / BOX)
    square = ((cycle + 1.0) / (1.5 * BOX)) ** 2
    rows.append(0.0197 / 2.0 * square)
    rows.append(np.exp(-10.0 * square))
    rows += [np.zeros(LANES)] * (-len(rows) % 8)
    swap = np.zeros((LANES, LANES))
    is_real = (lane // CYCLES) % 2 == 0
    swap[lane ^ CYCLES, lane] = np.where(is_real, -1.0, 1.0)
    return np.stack(rows).astype(np.float32), swap


def spread_kernel(copies, ref_ref, out_ref, rows):
    owned = ref_ref.shape[0]
    blocks = ref_ref.shape[1] // LANES
    for o in range(owned):
        row = ref_ref[o : o + 1, :].astype(F32)
        base = o * CHUNK
        for j in range(blocks):
            rows[base + j : base + j + 1, :] = row[:, j * LANES : (j + 1) * LANES]
        rows[base + blocks : base + CHUNK, :] = jnp.zeros((CHUNK - blocks, LANES), F32)
    one = rows[...]
    out_ref[...] = jnp.concatenate([one] * copies, axis=0).astype(BF16)


def prepare_kernel(x_ref, off_ref, grp_ref, noise_ref, table_ref, swap_ref, adj_ref, turned_ref, power_ref):
    rows = x_ref.shape[0]
    noise = jnp.concatenate([noise_ref[...]] * (LANES // CYCLES), axis=1)
    defocus = 10000.0 + 1500.0 * grp_ref[...].astype(F32)
    chi_cos, chi_sin = turn_trig(defocus * table_ref[2 * HALF : 2 * HALF + 1, :])
    ctf = -(0.995 * chi_sin + 0.1 * chi_cos) * table_ref[2 * HALF + 1 : 2 * HALF + 2, :]
    scale = ctf / noise
    power_ref[...] = ctf * scale
    shift = off_ref[...].astype(F32)
    shift_x = jnp.broadcast_to(shift[:, 0:1], (rows, LANES))
    shift_y = jnp.broadcast_to(shift[:, 1:2], (rows, LANES))
    swap = swap_ref[...]
    for t in range(HALF):
        turns = shift_x * table_ref[t : t + 1, :] + shift_y * table_ref[HALF + t : HALF + t + 1, :]
        cosine, sine = turn_trig(turns)
        cosine = cosine * scale
        sine = sine * scale
        for tile, sign in ((t, 1), (t + HALF, -1)):
            x = x_ref[:, tile * LANES : (tile + 1) * LANES]
            other = jnp.dot(x, swap, preferred_element_type=F32)
            first = x.astype(F32) * cosine
            second = other * sine
            out = first + second if sign > 0 else first - second
            adj_ref[:, tile * LANES : (tile + 1) * LANES] = out.astype(BF16)
            turned_ref[tile * LANES : (tile + 1) * LANES, :] = out.T.astype(BF16)


def score_kernel(got_ref, turned_ref, power_ref, prior_ref, e_ref, best_ref, lse_ref, wide):
    classes = prior_ref.shape[0]
    particles = turned_ref.shape[1]
    wide[...] = got_ref[...].astype(F32)
    blocks = []
    ref_power = jnp.zeros((classes, LANES), F32)
    for j in range(ROT):
        block = wide[pl.ds(j, classes, stride=CHUNK), :]
        ref_power = ref_power + block * block
        blocks.append(block.astype(BF16))
    energy = 0.5 * lax.dot_general(
        ref_power, power_ref[...], (((1,), (1,)), ((), ())), precision=HIGHEST, preferred_element_type=F32
    )
    bias = prior_ref[...] - energy
    bias = jnp.concatenate([bias, bias], axis=1)
    lhs = jnp.concatenate(
        [jnp.concatenate([blocks[(i + 2 * r) % ROT] for i in range(ROT)], axis=1) for r in range(HALF)], axis=0
    )
    tiles = [turned_ref[i * LANES : (i + 1) * LANES, :] for i in range(ROT)]
    rhs = jnp.concatenate([jnp.concatenate([tiles[i], tiles[i - 1]], axis=1) for i in range(ROT)], axis=0)
    raw = jnp.dot(lhs, rhs, preferred_element_type=F32).reshape(HALF, classes, 2 * particles)
    scores = raw + bias[None]
    best = jnp.max(jnp.max(scores, axis=0), axis=0, keepdims=True)
    best = jnp.maximum(best[:, :particles], best[:, particles:])
    both = jnp.concatenate([best, best], axis=1)
    e = jnp.exp(scores - both[None])
    total = jnp.sum(jnp.sum(e, axis=0), axis=0, keepdims=True)
    total = total[:, :particles] + total[:, particles:]
    e_ref[...] = e.reshape(HALF * classes, 2 * particles)
    best_ref[...] = best
    lse_ref[...] = best + jnp.log(total)


def sum_kernel(e_ref, best_ref, lse_ref, adj_ref, power_ref, out_ref, evidence_ref, wide):
    particles = adj_ref.shape[0]
    classes = e_ref.shape[0] // HALF
    lse = lse_ref[...]
    top = jnp.max(lse, axis=0, keepdims=True)
    evidence = top + jnp.log(jnp.sum(jnp.exp(lse - top), axis=0, keepdims=True))
    evidence_ref[...] = evidence
    factor = jnp.exp(best_ref[...] - evidence)
    post = e_ref[...] * jnp.concatenate([factor, factor], axis=1)
    mass = jnp.sum(post.reshape(HALF, classes, 2 * particles), axis=0)
    mass = mass[:, :particles] + mass[:, particles:]
    weight = jnp.dot(mass, power_ref[...], precision=HIGHEST, preferred_element_type=F32)
    post = post.astype(BF16)
    blocks = [
        post[(q // 2) * classes : (q // 2 + 1) * classes, (q % 2) * particles : (q % 2 + 1) * particles]
        for q in range(ROT)
    ]
    lhs = jnp.concatenate(
        [jnp.concatenate([blocks[(2 * r - i) % ROT] for i in range(ROT)], axis=1) for r in range(HALF)], axis=0
    )
    tiles = [adj_ref[:, i * LANES : (i + 1) * LANES] for i in range(ROT)]
    rhs = jnp.concatenate(
        [jnp.concatenate([tiles[i], tiles[(i + 1) % ROT]], axis=1) for i in range(ROT)], axis=0
    )
    data = jnp.dot(lhs, rhs, preferred_element_type=F32)
    for n in range(ROT):
        r, d = n // 2, n % 2
        wide[pl.ds(n, classes, stride=CHUNK), :] = data[r * classes : (r + 1) * classes, d * LANES : (d + 1) * LANES]
    group = lax.broadcasted_iota(jnp.int32, weight.shape, 1) // CYCLES
    high = weight.astype(BF16).astype(F32)
    rest = weight - high
    middle = rest.astype(BF16).astype(F32)
    terms = jnp.where(group == 0, high, jnp.where(group == 1, middle, jnp.where(group == 2, rest - middle, 0.0)))
    wide[pl.ds(ROT, classes, stride=CHUNK), :] = terms
    for n in range(ROT + 1, CHUNK):
        wide[pl.ds(n, classes, stride=CHUNK), :] = jnp.zeros((classes, LANES), F32)
    out_ref[...] = wide[...].astype(BF16)


def final_kernel(senders, got_ref, data_ref, weight_ref):
    owned = data_ref.shape[0]
    got = got_ref[...].astype(F32).reshape(senders, owned * CHUNK, LANES)
    total = jnp.sum(got, axis=0)
    for o in range(owned):
        base = o * CHUNK
        for n in range(ROT):
            data_ref[o : o + 1, n * LANES : (n + 1) * LANES] = total[base + n : base + n + 1, :]
        terms = total[base + ROT : base + ROT + 1, :]
        weight_ref[o : o + 1, :] = (
            terms[:, :CYCLES] + terms[:, CYCLES : 2 * CYCLES] + terms[:, 2 * CYCLES : 3 * CYCLES]
        )


def call(kernel, outs, scratch=(), flops=0, bytes_accessed=0):
    return pl.pallas_call(
        kernel,
        out_shape=tuple(jax.ShapeDtypeStruct(shape, dtype) for shape, dtype in outs),
        out_specs=tuple(pl.BlockSpec(memory_space=pltpu.VMEM) for _ in outs),
        scratch_shapes=list(scratch),
        compiler_params=pltpu.CompilerParams(vmem_limit_bytes=VMEM_LIMIT),
        cost_estimate=pl.CostEstimate(flops=flops, bytes_accessed=bytes_accessed, transcendentals=0),
    )


def per_device(particles, references, log_prior, noise_var, offsets, groups):
    dom_size = lax.axis_size("dom")
    cls_size = lax.axis_size("cls")
    rows, samples = particles.shape
    owned = references.shape[0]
    classes = log_prior.shape[0]
    message = classes * CHUNK
    table, swap = lane_tables()

    (spread,) = call(
        functools.partial(spread_kernel, dom_size),
        [((message, LANES), BF16)],
        [pltpu.VMEM((owned * CHUNK, LANES), F32)],
        bytes_accessed=message * LANES * 2,
    )(references)
    got = lax.all_to_all(spread, "dom", 0, 0, tiled=True)
    adjusted, turned, power = call(
        prepare_kernel,
        [((rows, samples), BF16), ((samples, rows), BF16), ((rows, LANES), F32)],
        flops=rows * samples * 300,
        bytes_accessed=rows * samples * 6,
    )(
        particles,
        offsets,
        groups.reshape(rows, 1),
        noise_var.reshape(1, CYCLES),
        jnp.asarray(table),
        jnp.asarray(swap, BF16),
    )
    dot_flops = 2 * ROT * classes * rows * samples
    e, best, lse = call(
        score_kernel,
        [((HALF * classes, 2 * rows), F32), ((1, rows), F32), ((1, rows), F32)],
        [pltpu.VMEM((message, LANES), F32)],
        flops=dot_flops,
        bytes_accessed=rows * samples * 4,
    )(got, turned, power, log_prior.reshape(classes, 1))
    lse_all = lax.all_gather(lse, "cls", axis=0, tiled=True)
    sums, evidence = call(
        sum_kernel,
        [((message, LANES), BF16), ((1, rows), F32)],
        [pltpu.VMEM((message, LANES), F32)],
        flops=dot_flops,
        bytes_accessed=rows * samples * 4,
    )(e, best, lse_all, adjusted, power)
    mine = lax.all_to_all(sums, "dom", 0, 0, tiled=True)
    data, weight = call(
        functools.partial(final_kernel, dom_size),
        [((owned, samples), F32), ((owned, CYCLES), F32)],
        bytes_accessed=message * LANES * 2,
    )(mine)
    return data, weight, evidence.reshape(rows)


def solution(mesh):
    return jax.shard_map(
        per_device,
        mesh=mesh,
        in_specs=(P("dom", None), P(("cls", "dom"), None), P("cls"), P(), P("dom", None), P("dom")),
        out_specs=(P(("cls", "dom"), None), P(("cls", "dom"), None), P("dom")),
        check_vma=False,
    )
```

```python
import functools
import math

import jax
import jax.numpy as jnp
import numpy as np
from jax import lax
from jax.experimental import pallas as pl
from jax.experimental.pallas import tpu as pltpu
from jax.sharding import PartitionSpec as P

BOX = 64
CYCLES = 32
ROT = 36
ANGLES = 72
LANES = 128
HALF = ROT // 2
GROUP = 3
CHUNK = 40
F32 = jnp.float32
BF16 = jnp.bfloat16
HIGHEST = lax.Precision.HIGHEST
VMEM_LIMIT = 24 * 1024 * 1024


def trig_polynomials():
    nodes = 0.125 + 0.125 * np.cos(np.pi * (np.arange(400) + 0.5) / 400)
    root = np.sqrt(nodes)
    fits = []
    for values, degree in ((np.cos(2 * np.pi * root), 7), (np.sin(2 * np.pi * root) / root, 7)):
        fit = np.polynomial.Chebyshev.fit(nodes, values, degree, domain=[0, 0.25])
        fits.append([float(c) for c in fit.convert(kind=np.polynomial.Polynomial).coef])
    return fits


COS_COEF, SIN_COEF = trig_polynomials()


def horner(coef, x):
    total = coef[-1] * x + coef[-2]
    for c in coef[-3::-1]:
        total = total * x + c
    return total


def turn_trig(turns):
    r = turns - jnp.floor(turns + 0.5)
    square = r * r
    return horner(COS_COEF, square), horner(SIN_COEF, square) * r


def lane_tables():
    lane = np.arange(LANES)
    cycle = lane % CYCLES
    rows = []
    for component in (np.cos, np.sin):
        for t in range(HALF):
            theta = 2.0 * np.pi * (2 * t + lane // 64) / ANGLES
            rows.append((cycle + 1.0) * component(theta) / BOX)
    square = ((cycle + 1.0) / (1.5 * BOX)) ** 2
    rows.append(0.0197 / 2.0 * square)
    rows.append(np.exp(-10.0 * square))
    rows += [np.zeros(LANES)] * (-len(rows) % 8)
    return np.stack(rows).astype(np.float32)


def spread_kernel(copies, ref_ref, out_ref, rows):
    owned = ref_ref.shape[0]
    blocks = ref_ref.shape[1] // LANES
    for o in range(owned):
        row = ref_ref[o : o + 1, :].astype(F32)
        base = o * CHUNK
        for j in range(blocks):
            rows[base + j : base + j + 1, :] = row[:, j * LANES : (j + 1) * LANES]
        rows[base + blocks : base + CHUNK, :] = jnp.zeros((CHUNK - blocks, LANES), F32)
    one = rows[...]
    out_ref[...] = jnp.concatenate([one] * copies, axis=0).astype(BF16)


def prepare_kernel(
    x_hbm, off_hbm, grp_hbm, noise_hbm, table_hbm, adj_ref, turned_ref, power_ref, x_ref, off_ref, grp_ref, noise_ref,
    table_ref, small_sems, x_sems
):
    rows = x_ref.shape[0]
    width = GROUP * LANES
    small = [
        pltpu.make_async_copy(source, target, small_sems.at[i])
        for i, (source, target) in enumerate(
            ((off_hbm, off_ref), (grp_hbm, grp_ref), (noise_hbm, noise_ref), (table_hbm, table_ref))
        )
    ]
    for copy in small:
        copy.start()
    parts = []
    for g in range(2 * HALF // GROUP):
        part = slice((g // 2 + g % 2 * (HALF // GROUP)) * width, (g // 2 + g % 2 * (HALF // GROUP) + 1) * width)
        copy = pltpu.make_async_copy(x_hbm.at[:, part], x_ref.at[:, part], x_sems.at[g])
        copy.start()
        parts.append(copy)
    out_lane = lax.broadcasted_iota(jnp.int32, (LANES, LANES), 1)
    in_lane = lax.broadcasted_iota(jnp.int32, (LANES, LANES), 0)
    is_real = (out_lane // CYCLES) % 2 == 0
    swap = jnp.where(
        is_real,
        jnp.where(in_lane == out_lane + CYCLES, -1.0, 0.0),
        jnp.where(in_lane == out_lane - CYCLES, 1.0, 0.0),
    ).astype(BF16)
    for copy in small:
        copy.wait()
    noise = jnp.concatenate([noise_ref[...]] * (LANES // CYCLES), axis=1)

    def down(row):
        return jnp.broadcast_to(row.astype(F32), (LANES, rows)).T

    defocus = 10000.0 + 1500.0 * down(grp_ref[...])
    chi_cos, chi_sin = turn_trig(defocus * table_ref[2 * HALF : 2 * HALF + 1, :])
    ctf = -(0.995 * chi_sin + 0.1 * chi_cos) * table_ref[2 * HALF + 1 : 2 * HALF + 2, :]
    scale = ctf / noise
    power_ref[...] = ctf * scale
    shift_x = down(off_ref[0:1, :])
    shift_y = down(off_ref[1:2, :])
    for t in range(HALF):
        if t % GROUP == 0:
            for copy in parts[2 * (t // GROUP) : 2 * (t // GROUP) + 2]:
                copy.wait()
        turns = shift_x * table_ref[t : t + 1, :] + shift_y * table_ref[HALF + t : HALF + t + 1, :]
        cosine, sine = turn_trig(turns)
        cosine = cosine * scale
        sine = sine * scale
        for tile, sign in ((t, 1), (t + HALF, -1)):
            x = x_ref[:, tile * LANES : (tile + 1) * LANES]
            other = jnp.dot(x, swap, preferred_element_type=F32)
            first = x.astype(F32) * cosine
            second = other * sine
            out = first + second if sign > 0 else first - second
            adj_ref[:, tile * LANES : (tile + 1) * LANES] = out.astype(BF16)
            turned_ref[tile * LANES : (tile + 1) * LANES, :] = out.T.astype(BF16)


def score_kernel(got_ref, turned_ref, power_ref, prior_ref, e_ref, best_ref, lse_ref, wide):
    classes = prior_ref.shape[1]
    particles = turned_ref.shape[1]
    diagonal = lax.broadcasted_iota(jnp.int32, (classes, classes), 0) == lax.broadcasted_iota(
        jnp.int32, (classes, classes), 1
    )
    prior = jnp.sum(jnp.where(diagonal, jnp.broadcast_to(prior_ref[...], (classes, classes)), 0.0), axis=1, keepdims=True)
    wide[...] = got_ref[...].astype(F32)
    blocks = []
    ref_power = jnp.zeros((classes, LANES), F32)
    for j in range(ROT):
        block = wide[pl.ds(j, classes, stride=CHUNK), :]
        ref_power = ref_power + block * block
        blocks.append(block.astype(BF16))
    energy = 0.5 * lax.dot_general(
        ref_power, power_ref[...], (((1,), (1,)), ((), ())), precision=HIGHEST, preferred_element_type=F32
    )
    bias = prior - energy
    bias = jnp.concatenate([bias, bias], axis=1)
    lhs = jnp.concatenate(
        [jnp.concatenate([blocks[(i + 2 * r) % ROT] for i in range(ROT)], axis=1) for r in range(HALF)], axis=0
    )
    tiles = [turned_ref[i * LANES : (i + 1) * LANES, :] for i in range(ROT)]
    rhs = jnp.concatenate([jnp.concatenate([tiles[i], tiles[i - 1]], axis=1) for i in range(ROT)], axis=0)
    raw = jnp.dot(lhs, rhs, preferred_element_type=F32).reshape(HALF, classes, 2 * particles)
    scores = raw + bias[None]
    best = jnp.max(jnp.max(scores, axis=0), axis=0, keepdims=True)
    best = jnp.maximum(best[:, :particles], best[:, particles:])
    both = jnp.concatenate([best, best], axis=1)
    e = jnp.exp(scores - both[None])
    total = jnp.sum(jnp.sum(e, axis=0), axis=0, keepdims=True)
    total = total[:, :particles] + total[:, particles:]
    e_ref[...] = e.reshape(HALF * classes, 2 * particles)
    best_ref[...] = best
    lse_ref[...] = best + jnp.log(total)


def sum_kernel(e_ref, best_ref, adj_ref, power_ref, *rest):
    *lse_refs, out_ref, evidence_ref, wide = rest
    particles = adj_ref.shape[0]
    classes = e_ref.shape[0] // HALF
    lse = jnp.concatenate([ref[...] for ref in lse_refs], axis=0)
    top = jnp.max(lse, axis=0, keepdims=True)
    evidence = top + jnp.log(jnp.sum(jnp.exp(lse - top), axis=0, keepdims=True))
    evidence_ref[...] = evidence
    factor = jnp.exp(best_ref[...] - evidence)
    post = e_ref[...] * jnp.concatenate([factor, factor], axis=1)
    mass = jnp.sum(post.reshape(HALF, classes, 2 * particles), axis=0)
    mass = mass[:, :particles] + mass[:, particles:]
    weight = jnp.dot(mass, power_ref[...], precision=HIGHEST, preferred_element_type=F32)
    post = post.astype(BF16)
    blocks = [
        post[(q // 2) * classes : (q // 2 + 1) * classes, (q % 2) * particles : (q % 2 + 1) * particles]
        for q in range(ROT)
    ]
    lhs = jnp.concatenate(
        [jnp.concatenate([blocks[(2 * r - i) % ROT] for i in range(ROT)], axis=1) for r in range(HALF)], axis=0
    )
    tiles = [adj_ref[:, i * LANES : (i + 1) * LANES] for i in range(ROT)]
    rhs = jnp.concatenate(
        [jnp.concatenate([tiles[i], tiles[(i + 1) % ROT]], axis=1) for i in range(ROT)], axis=0
    )
    data = jnp.dot(lhs, rhs, preferred_element_type=F32)
    for n in range(ROT):
        r, d = n // 2, n % 2
        wide[pl.ds(n, classes, stride=CHUNK), :] = data[r * classes : (r + 1) * classes, d * LANES : (d + 1) * LANES]
    group = lax.broadcasted_iota(jnp.int32, weight.shape, 1) // CYCLES
    high = weight.astype(BF16).astype(F32)
    rest = weight - high
    middle = rest.astype(BF16).astype(F32)
    terms = jnp.where(group == 0, high, jnp.where(group == 1, middle, jnp.where(group == 2, rest - middle, 0.0)))
    wide[pl.ds(ROT, classes, stride=CHUNK), :] = terms
    for n in range(ROT + 1, CHUNK):
        wide[pl.ds(n, classes, stride=CHUNK), :] = jnp.zeros((classes, LANES), F32)
    out_ref[...] = wide[...].astype(BF16)


def final_kernel(senders, got_ref, data_ref, weight_ref):
    owned = data_ref.shape[0]
    got = got_ref[...].astype(F32).reshape(senders, owned * CHUNK, LANES)
    total = jnp.sum(got, axis=0)
    for o in range(owned):
        base = o * CHUNK
        for n in range(ROT):
            data_ref[o : o + 1, n * LANES : (n + 1) * LANES] = total[base + n : base + n + 1, :]
        terms = total[base + ROT : base + ROT + 1, :]
        weight_ref[o : o + 1, :] = (
            terms[:, :CYCLES] + terms[:, CYCLES : 2 * CYCLES] + terms[:, 2 * CYCLES : 3 * CYCLES]
        )


def call(kernel, outs, scratch=(), in_hbm=(), flops=0, bytes_accessed=0):
    def run(*args):
        args = [pltpu.with_memory_space_constraint(x, pltpu.HBM) if i in in_hbm else x for i, x in enumerate(args)]
        return pl.pallas_call(
            kernel,
            out_shape=tuple(jax.ShapeDtypeStruct(shape, dtype) for shape, dtype in outs),
            in_specs=[pl.BlockSpec(memory_space=pltpu.HBM if i in in_hbm else pltpu.VMEM) for i in range(len(args))],
            out_specs=tuple(pl.BlockSpec(memory_space=pltpu.VMEM) for _ in outs),
            scratch_shapes=list(scratch),
            compiler_params=pltpu.CompilerParams(vmem_limit_bytes=VMEM_LIMIT),
            cost_estimate=pl.CostEstimate(flops=flops, bytes_accessed=bytes_accessed, transcendentals=0),
        )(*args)

    return run


def per_device(particles, references, log_prior, noise_var, offsets, groups):
    dom_size = lax.axis_size("dom")
    cls_size = lax.axis_size("cls")
    rows, samples = particles.shape
    owned = references.shape[0]
    classes = log_prior.shape[0]
    message = classes * CHUNK
    table = lane_tables()

    (spread,) = call(
        functools.partial(spread_kernel, dom_size),
        [((message, LANES), BF16)],
        [pltpu.VMEM((owned * CHUNK, LANES), F32)],
        bytes_accessed=message * LANES * 2,
    )(references)
    got = lax.all_to_all(spread, "dom", 0, 0, tiled=True)
    adjusted, turned, power = call(
        prepare_kernel,
        [((rows, samples), BF16), ((samples, rows), BF16), ((rows, LANES), F32)],
        [
            pltpu.VMEM((rows, samples), BF16),
            pltpu.VMEM((2, rows), jnp.int32),
            pltpu.VMEM((1, rows), jnp.int32),
            pltpu.VMEM((1, CYCLES), F32),
            pltpu.VMEM(table.shape, F32),
            pltpu.SemaphoreType.DMA((4,)),
            pltpu.SemaphoreType.DMA((2 * HALF // GROUP,)),
        ],
        in_hbm=range(5),
        flops=rows * samples * 300,
        bytes_accessed=rows * samples * 6,
    )(particles, offsets.T, groups.reshape(1, rows), noise_var.reshape(1, CYCLES), jnp.asarray(table))
    dot_flops = 2 * ROT * classes * rows * samples
    e, best, lse = call(
        score_kernel,
        [((HALF * classes, 2 * rows), F32), ((1, rows), F32), ((1, rows), F32)],
        [pltpu.VMEM((message, LANES), F32)],
        flops=dot_flops,
        bytes_accessed=rows * samples * 4,
    )(got, turned, power, log_prior.reshape(1, classes))
    if cls_size == 2:
        all_lse = (lse, lax.ppermute(lse, "cls", [(0, 1), (1, 0)]))
    else:
        all_lse = (lax.all_gather(lse, "cls", axis=0, tiled=True),)
    sums, evidence = call(
        sum_kernel,
        [((message, LANES), BF16), ((1, rows), F32)],
        [pltpu.VMEM((message, LANES), F32)],
        flops=dot_flops,
        bytes_accessed=rows * samples * 4,
    )(e, best, adjusted, power, *all_lse)
    mine = lax.all_to_all(sums, "dom", 0, 0, tiled=True)
    data, weight = call(
        functools.partial(final_kernel, dom_size),
        [((owned, samples), F32), ((owned, CYCLES), F32)],
        bytes_accessed=message * LANES * 2,
    )(mine)
    return data, weight, evidence.reshape(rows)


def solution(mesh):
    return jax.shard_map(
        per_device,
        mesh=mesh,
        in_specs=(P("dom", None), P(("cls", "dom"), None), P("cls"), P(), P("dom", None), P("dom")),
        out_specs=(P(("cls", "dom"), None), P(("cls", "dom"), None), P("dom")),
        check_vma=False,
    )
```

```python
import functools
import math

import jax
import jax.numpy as jnp
import numpy as np
from jax import lax
from jax.experimental import pallas as pl
from jax.experimental.pallas import tpu as pltpu
from jax.sharding import PartitionSpec as P

BOX = 64
CYCLES = 32
ROT = 36
ANGLES = 72
LANES = 128
HALF = ROT // 2
GROUP = 3
CHUNK = 40
F32 = jnp.float32
BF16 = jnp.bfloat16
HIGHEST = lax.Precision.HIGHEST
VMEM_LIMIT = 24 * 1024 * 1024


def trig_polynomials():
    nodes = 0.125 + 0.125 * np.cos(np.pi * (np.arange(400) + 0.5) / 400)
    root = np.sqrt(nodes)
    fits = []
    for values, degree in ((np.cos(2 * np.pi * root), 7), (np.sin(2 * np.pi * root) / root, 7)):
        fit = np.polynomial.Chebyshev.fit(nodes, values, degree, domain=[0, 0.25])
        fits.append([float(c) for c in fit.convert(kind=np.polynomial.Polynomial).coef])
    return fits


COS_COEF, SIN_COEF = trig_polynomials()


def horner(coef, x):
    total = coef[-1] * x + coef[-2]
    for c in coef[-3::-1]:
        total = total * x + c
    return total


def turn_trig(turns):
    r = turns - jnp.floor(turns + 0.5)
    square = r * r
    return horner(COS_COEF, square), horner(SIN_COEF, square) * r


def lane_tables():
    lane = np.arange(LANES)
    cycle = lane % CYCLES
    rows = []
    for component in (np.cos, np.sin):
        for t in range(HALF):
            theta = 2.0 * np.pi * (2 * t + lane // 64) / ANGLES
            rows.append((cycle + 1.0) * component(theta) / BOX)
    square = ((cycle + 1.0) / (1.5 * BOX)) ** 2
    rows.append(0.0197 / 2.0 * square)
    rows.append(np.exp(-10.0 * square))
    rows += [np.zeros(LANES)] * (-len(rows) % 8)
    return np.stack(rows).astype(np.float32)


def spread_kernel(ref_hbm, out_hbm, ref, rows, packed, in_sem, out_sems):
    copy = pltpu.make_async_copy(ref_hbm, ref, in_sem)
    copy.start()
    owned = ref.shape[0]
    blocks = ref.shape[1] // LANES
    for o in range(owned):
        rows[o * CHUNK + blocks : (o + 1) * CHUNK, :] = jnp.zeros((CHUNK - blocks, LANES), F32)
    copy.wait()
    for o in range(owned):
        row = ref[o : o + 1, :].astype(F32)
        for j in range(blocks):
            rows[o * CHUNK + j : o * CHUNK + j + 1, :] = row[:, j * LANES : (j + 1) * LANES]
    unit = packed.shape[0]
    packed[...] = jnp.concatenate([rows[...]] * (unit // rows.shape[0]), axis=0).astype(BF16)
    copies = [
        pltpu.make_async_copy(packed, out_hbm.at[i * unit : (i + 1) * unit, :], out_sems.at[i])
        for i in range(out_hbm.shape[0] // unit)
    ]
    for copy in copies:
        copy.start()
    for copy in copies:
        copy.wait()


def prepare_kernel(
    x_hbm, off_hbm, grp_hbm, noise_hbm, table_hbm, adj_ref, turned_ref, power_ref, x_ref, off_ref, grp_ref, noise_ref,
    table_ref, small_sems, x_sems
):
    rows = x_ref.shape[0]
    width = GROUP * LANES
    small = [
        pltpu.make_async_copy(source, target, small_sems.at[i])
        for i, (source, target) in enumerate(
            ((off_hbm, off_ref), (grp_hbm, grp_ref), (noise_hbm, noise_ref), (table_hbm, table_ref))
        )
    ]
    for copy in small:
        copy.start()
    parts = []
    for g in range(2 * HALF // GROUP):
        part = slice((g // 2 + g % 2 * (HALF // GROUP)) * width, (g // 2 + g % 2 * (HALF // GROUP) + 1) * width)
        copy = pltpu.make_async_copy(x_hbm.at[:, part], x_ref.at[:, part], x_sems.at[g])
        copy.start()
        parts.append(copy)
    out_lane = lax.broadcasted_iota(jnp.int32, (LANES, LANES), 1)
    in_lane = lax.broadcasted_iota(jnp.int32, (LANES, LANES), 0)
    is_real = (out_lane // CYCLES) % 2 == 0
    swap = jnp.where(
        is_real,
        jnp.where(in_lane == out_lane + CYCLES, -1.0, 0.0),
        jnp.where(in_lane == out_lane - CYCLES, 1.0, 0.0),
    ).astype(BF16)
    for copy in small:
        copy.wait()
    noise = jnp.concatenate([noise_ref[...]] * (LANES // CYCLES), axis=1)

    def down(row):
        return jnp.broadcast_to(row.astype(F32), (LANES, rows)).T

    defocus = 10000.0 + 1500.0 * down(grp_ref[...])
    chi_cos, chi_sin = turn_trig(defocus * table_ref[2 * HALF : 2 * HALF + 1, :])
    ctf = -(0.995 * chi_sin + 0.1 * chi_cos) * table_ref[2 * HALF + 1 : 2 * HALF + 2, :]
    scale = ctf / noise
    power_ref[...] = ctf * scale
    shift_x = down(off_ref[0:1, :])
    shift_y = down(off_ref[1:2, :])
    for t in range(HALF):
        if t % GROUP == 0:
            for copy in parts[2 * (t // GROUP) : 2 * (t // GROUP) + 2]:
                copy.wait()
        turns = shift_x * table_ref[t : t + 1, :] + shift_y * table_ref[HALF + t : HALF + t + 1, :]
        cosine, sine = turn_trig(turns)
        cosine = cosine * scale
        sine = sine * scale
        for tile, sign in ((t, 1), (t + HALF, -1)):
            x = x_ref[:, tile * LANES : (tile + 1) * LANES]
            other = jnp.dot(x, swap, preferred_element_type=F32)
            first = x.astype(F32) * cosine
            second = other * sine
            out = first + second if sign > 0 else first - second
            adj_ref[:, tile * LANES : (tile + 1) * LANES] = out.astype(BF16)
            turned_ref[tile * LANES : (tile + 1) * LANES, :] = out.T.astype(BF16)


def score_kernel(first, got_ref, turned_ref, power_ref, prior_ref, e_ref, best_ref, lse_ref, wide):
    classes = prior_ref.shape[1]
    particles = turned_ref.shape[1]
    place = lax.broadcasted_iota(jnp.int32, (classes, classes), 0) + first
    place = jnp.where(place >= classes, place - classes, place)
    held = place == lax.broadcasted_iota(jnp.int32, (classes, classes), 1)
    prior = jnp.sum(jnp.where(held, jnp.broadcast_to(prior_ref[...], (classes, classes)), 0.0), axis=1, keepdims=True)
    wide[...] = got_ref[...].astype(F32)
    blocks = []
    ref_power = jnp.zeros((classes, LANES), F32)
    for j in range(ROT):
        block = wide[pl.ds(j, classes, stride=CHUNK), :]
        ref_power = ref_power + block * block
        blocks.append(block.astype(BF16))
    energy = 0.5 * lax.dot_general(
        ref_power, power_ref[...], (((1,), (1,)), ((), ())), precision=HIGHEST, preferred_element_type=F32
    )
    bias = prior - energy
    bias = jnp.concatenate([bias, bias], axis=1)
    lhs = jnp.concatenate(
        [jnp.concatenate([blocks[(i + 2 * r) % ROT] for i in range(ROT)], axis=1) for r in range(HALF)], axis=0
    )
    tiles = [turned_ref[i * LANES : (i + 1) * LANES, :] for i in range(ROT)]
    rhs = jnp.concatenate([jnp.concatenate([tiles[i], tiles[i - 1]], axis=1) for i in range(ROT)], axis=0)
    raw = jnp.dot(lhs, rhs, preferred_element_type=F32).reshape(HALF, classes, 2 * particles)
    scores = raw + bias[None]
    best = jnp.max(jnp.max(scores, axis=0), axis=0, keepdims=True)
    best = jnp.maximum(best[:, :particles], best[:, particles:])
    both = jnp.concatenate([best, best], axis=1)
    e = jnp.exp(scores - both[None])
    total = jnp.sum(jnp.sum(e, axis=0), axis=0, keepdims=True)
    total = total[:, :particles] + total[:, particles:]
    e_ref[...] = e.reshape(HALF * classes, 2 * particles)
    best_ref[...] = best
    lse_ref[...] = best + jnp.log(total)


def sum_kernel(e_ref, best_ref, adj_ref, power_ref, *rest):
    *lse_refs, out_ref, evidence_ref, wide = rest
    particles = adj_ref.shape[0]
    classes = e_ref.shape[0] // HALF
    lse = jnp.concatenate([ref[...] for ref in lse_refs], axis=0)
    top = jnp.max(lse, axis=0, keepdims=True)
    evidence = top + jnp.log(jnp.sum(jnp.exp(lse - top), axis=0, keepdims=True))
    evidence_ref[...] = evidence
    factor = jnp.exp(best_ref[...] - evidence)
    post = e_ref[...] * jnp.concatenate([factor, factor], axis=1)
    mass = jnp.sum(post.reshape(HALF, classes, 2 * particles), axis=0)
    mass = mass[:, :particles] + mass[:, particles:]
    weight = jnp.dot(mass, power_ref[...], precision=HIGHEST, preferred_element_type=F32)
    post = post.astype(BF16)
    blocks = [
        post[(q // 2) * classes : (q // 2 + 1) * classes, (q % 2) * particles : (q % 2 + 1) * particles]
        for q in range(ROT)
    ]
    lhs = jnp.concatenate(
        [jnp.concatenate([blocks[(2 * r - i) % ROT] for i in range(ROT)], axis=1) for r in range(HALF)], axis=0
    )
    tiles = [adj_ref[:, i * LANES : (i + 1) * LANES] for i in range(ROT)]
    rhs = jnp.concatenate(
        [jnp.concatenate([tiles[i], tiles[(i + 1) % ROT]], axis=1) for i in range(ROT)], axis=0
    )
    data = jnp.dot(lhs, rhs, preferred_element_type=F32)
    for n in range(ROT):
        r, d = n // 2, n % 2
        wide[pl.ds(n, classes, stride=CHUNK), :] = data[r * classes : (r + 1) * classes, d * LANES : (d + 1) * LANES]
    group = lax.broadcasted_iota(jnp.int32, weight.shape, 1) // CYCLES
    high = weight.astype(BF16).astype(F32)
    rest = weight - high
    middle = rest.astype(BF16).astype(F32)
    terms = jnp.where(group == 0, high, jnp.where(group == 1, middle, jnp.where(group == 2, rest - middle, 0.0)))
    wide[pl.ds(ROT, classes, stride=CHUNK), :] = terms
    for n in range(ROT + 1, CHUNK):
        wide[pl.ds(n, classes, stride=CHUNK), :] = jnp.zeros((classes, LANES), F32)
    out_ref[...] = wide[...].astype(BF16)


def final_kernel(senders, got_ref, data_ref, weight_ref):
    owned = data_ref.shape[0]
    got = got_ref[...].astype(F32).reshape(senders, owned * CHUNK, LANES)
    total = jnp.sum(got, axis=0)
    for o in range(owned):
        base = o * CHUNK
        for n in range(ROT):
            data_ref[o : o + 1, n * LANES : (n + 1) * LANES] = total[base + n : base + n + 1, :]
        terms = total[base + ROT : base + ROT + 1, :]
        weight_ref[o : o + 1, :] = (
            terms[:, :CYCLES] + terms[:, CYCLES : 2 * CYCLES] + terms[:, 2 * CYCLES : 3 * CYCLES]
        )


def call(kernel, outs, scratch=(), in_hbm=(), out_space=pltpu.VMEM, flops=0, bytes_accessed=0):
    def run(*args):
        args = [pltpu.with_memory_space_constraint(x, pltpu.HBM) if i in in_hbm else x for i, x in enumerate(args)]
        return pl.pallas_call(
            kernel,
            out_shape=tuple(jax.ShapeDtypeStruct(shape, dtype) for shape, dtype in outs),
            in_specs=[pl.BlockSpec(memory_space=pltpu.HBM if i in in_hbm else pltpu.VMEM) for i in range(len(args))],
            out_specs=tuple(pl.BlockSpec(memory_space=out_space) for _ in outs),
            scratch_shapes=list(scratch),
            compiler_params=pltpu.CompilerParams(vmem_limit_bytes=VMEM_LIMIT),
            cost_estimate=pl.CostEstimate(flops=flops, bytes_accessed=bytes_accessed, transcendentals=0),
        )(*args)

    return run


def per_device(particles, references, log_prior, noise_var, offsets, groups):
    dom_size = lax.axis_size("dom")
    cls_size = lax.axis_size("cls")
    rows, samples = particles.shape
    owned = references.shape[0]
    classes = log_prior.shape[0]
    message = classes * CHUNK
    table = lane_tables()

    root = dom_size * 3 // 4 - 1
    exchange = functools.partial(
        lax.all_to_all,
        axis_name="dom",
        split_axis=0,
        concat_axis=0,
        axis_index_groups=[[(i + root) % dom_size for i in range(dom_size)]],
        tiled=True,
    )
    unit = math.lcm(owned * CHUNK, 16)
    (spread,) = call(
        spread_kernel,
        [((message, LANES), BF16)],
        [
            pltpu.VMEM((owned, samples), BF16),
            pltpu.VMEM((owned * CHUNK, LANES), F32),
            pltpu.VMEM((unit, LANES), BF16),
            pltpu.SemaphoreType.DMA,
            pltpu.SemaphoreType.DMA((message // unit,)),
        ],
        in_hbm=(0,),
        out_space=pl.ANY,
        bytes_accessed=message * LANES * 2,
    )(references)
    got = exchange(spread)
    adjusted, turned, power = call(
        prepare_kernel,
        [((rows, samples), BF16), ((samples, rows), BF16), ((rows, LANES), F32)],
        [
            pltpu.VMEM((rows, samples), BF16),
            pltpu.VMEM((2, rows), jnp.int32),
            pltpu.VMEM((1, rows), jnp.int32),
            pltpu.VMEM((1, CYCLES), F32),
            pltpu.VMEM(table.shape, F32),
            pltpu.SemaphoreType.DMA((4,)),
            pltpu.SemaphoreType.DMA((2 * HALF // GROUP,)),
        ],
        in_hbm=range(5),
        flops=rows * samples * 300,
        bytes_accessed=rows * samples * 6,
    )(particles, offsets.T, groups.reshape(1, rows), noise_var.reshape(1, CYCLES), jnp.asarray(table))
    dot_flops = 2 * ROT * classes * rows * samples
    e, best, lse = call(
        functools.partial(score_kernel, root * owned),
        [((HALF * classes, 2 * rows), F32), ((1, rows), F32), ((1, rows), F32)],
        [pltpu.VMEM((message, LANES), F32)],
        flops=dot_flops,
        bytes_accessed=rows * samples * 4,
    )(got, turned, power, log_prior.reshape(1, classes))
    if cls_size == 2:
        all_lse = (lse, lax.ppermute(lse, "cls", [(0, 1), (1, 0)]))
    else:
        all_lse = (lax.all_gather(lse, "cls", axis=0, tiled=True),)
    sums, evidence = call(
        sum_kernel,
        [((message, LANES), BF16), ((1, rows), F32)],
        [pltpu.VMEM((message, LANES), F32)],
        flops=dot_flops,
        bytes_accessed=rows * samples * 4,
    )(e, best, adjusted, power, *all_lse)
    mine = exchange(sums)
    data, weight = call(
        functools.partial(final_kernel, dom_size),
        [((owned, samples), F32), ((owned, CYCLES), F32)],
        bytes_accessed=message * LANES * 2,
    )(mine)
    return data, weight, evidence.reshape(rows)


def solution(mesh):
    return jax.shard_map(
        per_device,
        mesh=mesh,
        in_specs=(P("dom", None), P(("cls", "dom"), None), P("cls"), P(), P("dom", None), P("dom")),
        out_specs=(P(("cls", "dom"), None), P(("cls", "dom"), None), P("dom")),
        check_vma=False,
    )
```

```python
import functools
import math

import jax
import jax.numpy as jnp
import numpy as np
from jax import lax
from jax.experimental import pallas as pl
from jax.experimental.pallas import tpu as pltpu
from jax.sharding import PartitionSpec as P

BOX = 64
CYCLES = 32
ROT = 36
ANGLES = 72
LANES = 128
HALF = ROT // 2
GROUP = 3
CHUNK = 40
ORDER = [11, 10, 0, 5, 6, 4, 14, 1, 15, 8, 13, 7, 3, 2, 12, 9]
F32 = jnp.float32
BF16 = jnp.bfloat16
HIGHEST = lax.Precision.HIGHEST
VMEM_LIMIT = 24 * 1024 * 1024


def trig_polynomials():
    nodes = 0.125 + 0.125 * np.cos(np.pi * (np.arange(400) + 0.5) / 400)
    root = np.sqrt(nodes)
    fits = []
    for values, degree in ((np.cos(2 * np.pi * root), 7), (np.sin(2 * np.pi * root) / root, 7)):
        fit = np.polynomial.Chebyshev.fit(nodes, values, degree, domain=[0, 0.25])
        fits.append([float(c) for c in fit.convert(kind=np.polynomial.Polynomial).coef])
    return fits


COS_COEF, SIN_COEF = trig_polynomials()


def horner(coef, x):
    total = coef[-1] * x + coef[-2]
    for c in coef[-3::-1]:
        total = total * x + c
    return total


def turn_trig(turns):
    r = turns - jnp.floor(turns + 0.5)
    square = r * r
    return horner(COS_COEF, square), horner(SIN_COEF, square) * r


def lane_tables():
    lane = np.arange(LANES)
    cycle = lane % CYCLES
    rows = []
    for component in (np.cos, np.sin):
        for t in range(HALF):
            theta = 2.0 * np.pi * (2 * t + lane // 64) / ANGLES
            rows.append((cycle + 1.0) * component(theta) / BOX)
    square = ((cycle + 1.0) / (1.5 * BOX)) ** 2
    rows.append(0.0197 / 2.0 * square)
    rows.append(np.exp(-10.0 * square))
    rows += [np.zeros(LANES)] * (-len(rows) % 8)
    return np.stack(rows).astype(np.float32)


def retile_kernel(ref_ref, out_ref, rows):
    owned = ref_ref.shape[0]
    blocks = ref_ref.shape[1] // LANES
    for o in range(owned):
        row = ref_ref[o : o + 1, :].astype(F32)
        for j in range(blocks):
            rows[o * CHUNK + j : o * CHUNK + j + 1, :] = row[:, j * LANES : (j + 1) * LANES]
        rows[o * CHUNK + blocks : (o + 1) * CHUNK, :] = jnp.zeros((CHUNK - blocks, LANES), F32)
    out_ref[...] = rows[...].astype(BF16)


def prepare_kernel(
    x_hbm, off_hbm, grp_hbm, noise_hbm, table_hbm, adj_ref, turned_ref, power_ref, x_ref, off_ref, grp_ref, noise_ref,
    table_ref, small_sems, x_sems
):
    rows = x_ref.shape[0]
    width = GROUP * LANES
    small = [
        pltpu.make_async_copy(source, target, small_sems.at[i])
        for i, (source, target) in enumerate(
            ((off_hbm, off_ref), (grp_hbm, grp_ref), (noise_hbm, noise_ref), (table_hbm, table_ref))
        )
    ]
    for copy in small:
        copy.start()
    parts = []
    for g in range(2 * HALF // GROUP):
        part = slice((g // 2 + g % 2 * (HALF // GROUP)) * width, (g // 2 + g % 2 * (HALF // GROUP) + 1) * width)
        copy = pltpu.make_async_copy(x_hbm.at[:, part], x_ref.at[:, part], x_sems.at[g])
        copy.start()
        parts.append(copy)
    out_lane = lax.broadcasted_iota(jnp.int32, (LANES, LANES), 1)
    in_lane = lax.broadcasted_iota(jnp.int32, (LANES, LANES), 0)
    is_real = (out_lane // CYCLES) % 2 == 0
    swap = jnp.where(
        is_real,
        jnp.where(in_lane == out_lane + CYCLES, -1.0, 0.0),
        jnp.where(in_lane == out_lane - CYCLES, 1.0, 0.0),
    ).astype(BF16)
    for copy in small:
        copy.wait()
    noise = jnp.concatenate([noise_ref[...]] * (LANES // CYCLES), axis=1)

    def down(row):
        return jnp.broadcast_to(row.astype(F32), (LANES, rows)).T

    defocus = 10000.0 + 1500.0 * down(grp_ref[...])
    chi_cos, chi_sin = turn_trig(defocus * table_ref[2 * HALF : 2 * HALF + 1, :])
    ctf = -(0.995 * chi_sin + 0.1 * chi_cos) * table_ref[2 * HALF + 1 : 2 * HALF + 2, :]
    scale = ctf / noise
    power_ref[...] = ctf * scale
    shift_x = down(off_ref[0:1, :])
    shift_y = down(off_ref[1:2, :])
    for t in range(HALF):
        if t % GROUP == 0:
            for copy in parts[2 * (t // GROUP) : 2 * (t // GROUP) + 2]:
                copy.wait()
        turns = shift_x * table_ref[t : t + 1, :] + shift_y * table_ref[HALF + t : HALF + t + 1, :]
        cosine, sine = turn_trig(turns)
        cosine = cosine * scale
        sine = sine * scale
        for tile, sign in ((t, 1), (t + HALF, -1)):
            x = x_ref[:, tile * LANES : (tile + 1) * LANES]
            other = jnp.dot(x, swap, preferred_element_type=F32)
            first = x.astype(F32) * cosine
            second = other * sine
            out = first + second if sign > 0 else first - second
            adj_ref[:, tile * LANES : (tile + 1) * LANES] = out.astype(BF16)
            turned_ref[tile * LANES : (tile + 1) * LANES, :] = out.T.astype(BF16)


def score_kernel(held, got_ref, turned_ref, power_ref, prior_ref, e_ref, best_ref, lse_ref, wide):
    classes = prior_ref.shape[1]
    particles = turned_ref.shape[1]
    row = lax.broadcasted_iota(jnp.int32, (classes, classes), 0)
    place = jnp.zeros((classes, classes), jnp.int32)
    for i, c in enumerate(held):
        place = jnp.where(row == i, c, place)
    diagonal = place == lax.broadcasted_iota(jnp.int32, (classes, classes), 1)
    prior = jnp.sum(jnp.where(diagonal, jnp.broadcast_to(prior_ref[...], (classes, classes)), 0.0), axis=1, keepdims=True)
    wide[...] = got_ref[...].astype(F32)
    blocks = []
    ref_power = jnp.zeros((classes, LANES), F32)
    for j in range(ROT):
        block = wide[pl.ds(j, classes, stride=CHUNK), :]
        ref_power = ref_power + block * block
        blocks.append(block.astype(BF16))
    energy = 0.5 * lax.dot_general(
        ref_power, power_ref[...], (((1,), (1,)), ((), ())), precision=HIGHEST, preferred_element_type=F32
    )
    bias = prior - energy
    bias = jnp.concatenate([bias, bias], axis=1)
    lhs = jnp.concatenate(
        [jnp.concatenate([blocks[(i + 2 * r) % ROT] for i in range(ROT)], axis=1) for r in range(HALF)], axis=0
    )
    tiles = [turned_ref[i * LANES : (i + 1) * LANES, :] for i in range(ROT)]
    rhs = jnp.concatenate([jnp.concatenate([tiles[i], tiles[i - 1]], axis=1) for i in range(ROT)], axis=0)
    raw = jnp.dot(lhs, rhs, preferred_element_type=F32).reshape(HALF, classes, 2 * particles)
    scores = raw + bias[None]
    best = jnp.max(jnp.max(scores, axis=0), axis=0, keepdims=True)
    best = jnp.maximum(best[:, :particles], best[:, particles:])
    both = jnp.concatenate([best, best], axis=1)
    e = jnp.exp(scores - both[None])
    total = jnp.sum(jnp.sum(e, axis=0), axis=0, keepdims=True)
    total = total[:, :particles] + total[:, particles:]
    e_ref[...] = e.reshape(HALF * classes, 2 * particles)
    best_ref[...] = best
    lse_ref[...] = best + jnp.log(total)


def total_evidence(lse_refs):
    lse = jnp.concatenate([ref[...] for ref in lse_refs], axis=0)
    top = jnp.max(lse, axis=0, keepdims=True)
    return top + jnp.log(jnp.sum(jnp.exp(lse - top), axis=0, keepdims=True))


def sum_kernel(e_ref, best_ref, adj_ref, power_ref, *rest):
    *lse_refs, out_ref, wide = rest
    particles = adj_ref.shape[0]
    classes = e_ref.shape[0] // HALF
    factor = jnp.exp(best_ref[...] - total_evidence(lse_refs))
    post = e_ref[...] * jnp.concatenate([factor, factor], axis=1)
    mass = jnp.sum(post.reshape(HALF, classes, 2 * particles), axis=0)
    mass = mass[:, :particles] + mass[:, particles:]
    weight = jnp.dot(mass, power_ref[...], precision=HIGHEST, preferred_element_type=F32)
    post = post.astype(BF16)
    blocks = [
        post[(q // 2) * classes : (q // 2 + 1) * classes, (q % 2) * particles : (q % 2 + 1) * particles]
        for q in range(ROT)
    ]
    lhs = jnp.concatenate(
        [jnp.concatenate([blocks[(2 * r - i) % ROT] for i in range(ROT)], axis=1) for r in range(HALF)], axis=0
    )
    tiles = [adj_ref[:, i * LANES : (i + 1) * LANES] for i in range(ROT)]
    rhs = jnp.concatenate(
        [jnp.concatenate([tiles[i], tiles[(i + 1) % ROT]], axis=1) for i in range(ROT)], axis=0
    )
    data = jnp.dot(lhs, rhs, preferred_element_type=F32)
    for n in range(ROT):
        r, d = n // 2, n % 2
        wide[pl.ds(n, classes, stride=CHUNK), :] = data[r * classes : (r + 1) * classes, d * LANES : (d + 1) * LANES]
    group = lax.broadcasted_iota(jnp.int32, weight.shape, 1) // CYCLES
    high = weight.astype(BF16).astype(F32)
    rest = weight - high
    middle = rest.astype(BF16).astype(F32)
    terms = jnp.where(group == 0, high, jnp.where(group == 1, middle, jnp.where(group == 2, rest - middle, 0.0)))
    wide[pl.ds(ROT, classes, stride=CHUNK), :] = terms
    for n in range(ROT + 1, CHUNK):
        wide[pl.ds(n, classes, stride=CHUNK), :] = jnp.zeros((classes, LANES), F32)
    out_ref[...] = wide[...].astype(BF16)


def final_kernel(senders, got_ref, *rest):
    *lse_refs, data_ref, weight_ref, evidence_ref = rest
    evidence_ref[...] = total_evidence(lse_refs)
    owned = data_ref.shape[0]
    got = got_ref[...].astype(F32).reshape(senders, owned * CHUNK, LANES)
    total = jnp.sum(got, axis=0)
    for o in range(owned):
        base = o * CHUNK
        for n in range(ROT):
            data_ref[o : o + 1, n * LANES : (n + 1) * LANES] = total[base + n : base + n + 1, :]
        terms = total[base + ROT : base + ROT + 1, :]
        weight_ref[o : o + 1, :] = (
            terms[:, :CYCLES] + terms[:, CYCLES : 2 * CYCLES] + terms[:, 2 * CYCLES : 3 * CYCLES]
        )


def call(kernel, outs, scratch=(), in_hbm=(), out_space=pltpu.VMEM, flops=0, bytes_accessed=0):
    def run(*args):
        args = [pltpu.with_memory_space_constraint(x, pltpu.HBM) if i in in_hbm else x for i, x in enumerate(args)]
        return pl.pallas_call(
            kernel,
            out_shape=tuple(jax.ShapeDtypeStruct(shape, dtype) for shape, dtype in outs),
            in_specs=[pl.BlockSpec(memory_space=pltpu.HBM if i in in_hbm else pltpu.VMEM) for i in range(len(args))],
            out_specs=tuple(pl.BlockSpec(memory_space=out_space) for _ in outs),
            scratch_shapes=list(scratch),
            compiler_params=pltpu.CompilerParams(vmem_limit_bytes=VMEM_LIMIT),
            cost_estimate=pl.CostEstimate(flops=flops, bytes_accessed=bytes_accessed, transcendentals=0),
        )(*args)

    return run


def exchange_order(dom_size):
    if dom_size == len(ORDER):
        return ORDER
    root = dom_size * 3 // 4 - 1
    return [(i + root) % dom_size for i in range(dom_size)]


def per_device(particles, references, log_prior, noise_var, offsets, groups):
    dom_size = lax.axis_size("dom")
    cls_size = lax.axis_size("cls")
    rows, samples = particles.shape
    owned = references.shape[0]
    classes = log_prior.shape[0]
    message = classes * CHUNK
    table = lane_tables()

    order = exchange_order(dom_size)
    exchange = functools.partial(
        lax.all_to_all,
        axis_name="dom",
        split_axis=0,
        concat_axis=0,
        axis_index_groups=[order],
        tiled=True,
    )
    (own,) = call(
        retile_kernel,
        [((owned * CHUNK, LANES), BF16)],
        [pltpu.VMEM((owned * CHUNK, LANES), F32)],
        bytes_accessed=message * LANES * 2,
    )(references)
    spread = jnp.broadcast_to(own[None], (dom_size, owned * CHUNK, LANES)).reshape(message, LANES)
    got = exchange(spread)
    adjusted, turned, power = call(
        prepare_kernel,
        [((rows, samples), BF16), ((samples, rows), BF16), ((rows, LANES), F32)],
        [
            pltpu.VMEM((rows, samples), BF16),
            pltpu.VMEM((2, rows), jnp.int32),
            pltpu.VMEM((1, rows), jnp.int32),
            pltpu.VMEM((1, CYCLES), F32),
            pltpu.VMEM(table.shape, F32),
            pltpu.SemaphoreType.DMA((4,)),
            pltpu.SemaphoreType.DMA((2 * HALF // GROUP,)),
        ],
        in_hbm=range(5),
        flops=rows * samples * 300,
        bytes_accessed=rows * samples * 6,
    )(particles, offsets.T, groups.reshape(1, rows), noise_var.reshape(1, CYCLES), jnp.asarray(table))
    dot_flops = 2 * ROT * classes * rows * samples
    e, best, lse = call(
        functools.partial(score_kernel, [d * owned + o for d in order for o in range(owned)]),
        [((HALF * classes, 2 * rows), F32), ((1, rows), F32), ((1, rows), F32)],
        [pltpu.VMEM((message, LANES), F32)],
        flops=dot_flops,
        bytes_accessed=rows * samples * 4,
    )(got, turned, power, log_prior.reshape(1, classes))
    if cls_size == 2:
        all_lse = (lse, lax.ppermute(lse, "cls", [(0, 1), (1, 0)]))
    else:
        all_lse = (lax.all_gather(lse, "cls", axis=0, tiled=True),)
    (sums,) = call(
        sum_kernel,
        [((message, LANES), BF16)],
        [pltpu.VMEM((message, LANES), F32)],
        flops=dot_flops,
        bytes_accessed=rows * samples * 4,
    )(e, best, adjusted, power, *all_lse)
    mine = exchange(sums)
    data, weight, evidence = call(
        functools.partial(final_kernel, dom_size),
        [((owned, samples), F32), ((owned, CYCLES), F32), ((1, rows), F32)],
        bytes_accessed=message * LANES * 2,
    )(mine, *all_lse)
    return data, weight, evidence.reshape(rows)


def solution(mesh):
    return jax.shard_map(
        per_device,
        mesh=mesh,
        in_specs=(P("dom", None), P(("cls", "dom"), None), P("cls"), P(), P("dom", None), P("dom")),
        out_specs=(P(("cls", "dom"), None), P(("cls", "dom"), None), P("dom")),
        check_vma=False,
    )
```

```python
import functools
import math

import jax
import jax.numpy as jnp
import numpy as np
from jax import lax
from jax.experimental import pallas as pl
from jax.experimental.pallas import tpu as pltpu
from jax.sharding import PartitionSpec as P

BOX = 64
CYCLES = 32
ROT = 36
ANGLES = 72
LANES = 128
HALF = ROT // 2
PARTS = 4
AHEAD = 6
CHUNK = 40
ORDER = [11, 10, 0, 5, 6, 4, 14, 1, 15, 8, 13, 7, 3, 2, 12, 9]
F32 = jnp.float32
BF16 = jnp.bfloat16
HIGHEST = lax.Precision.HIGHEST
VMEM_LIMIT = 24 * 1024 * 1024


def trig_polynomials():
    nodes = 0.125 + 0.125 * np.cos(np.pi * (np.arange(400) + 0.5) / 400)
    root = np.sqrt(nodes)
    fits = []
    for values, degree in ((np.cos(2 * np.pi * root), 6), (np.sin(2 * np.pi * root) / root, 5)):
        fit = np.polynomial.Chebyshev.fit(nodes, values, degree, domain=[0, 0.25])
        fits.append([float(c) for c in fit.convert(kind=np.polynomial.Polynomial).coef])
    return fits


COS_COEF, SIN_COEF = trig_polynomials()


def horner(coef, x):
    total = coef[-1] * x + coef[-2]
    for c in coef[-3::-1]:
        total = total * x + c
    return total


def turn_trig(turns):
    r = turns - jnp.floor(turns + 0.5)
    square = r * r
    return horner(COS_COEF, square), horner(SIN_COEF, square) * r


def lane_tables():
    lane = np.arange(LANES)
    cycle = lane % CYCLES
    rows = []
    for component in (np.cos, np.sin):
        for t in range(HALF):
            theta = 2.0 * np.pi * (2 * t + lane // 64) / ANGLES
            rows.append((cycle + 1.0) * component(theta) / BOX)
    square = ((cycle + 1.0) / (1.5 * BOX)) ** 2
    rows.append(0.0197 / 2.0 * square)
    rows.append(np.exp(-10.0 * square))
    rows += [np.zeros(LANES)] * (-len(rows) % 8)
    return np.stack(rows).astype(np.float32)


def retile_kernel(ref_ref, out_ref, rows):
    owned = ref_ref.shape[0]
    blocks = ref_ref.shape[1] // LANES
    for o in range(owned):
        row = ref_ref[o : o + 1, :].astype(F32)
        for j in range(blocks):
            rows[o * CHUNK + j : o * CHUNK + j + 1, :] = row[:, j * LANES : (j + 1) * LANES]
        rows[o * CHUNK + blocks : (o + 1) * CHUNK, :] = jnp.zeros((CHUNK - blocks, LANES), F32)
    out_ref[...] = rows[...].astype(BF16)


def prepare_kernel(
    x_hbm, off_hbm, grp_hbm, noise_hbm, table_hbm, adj_ref, turned_ref, power_ref, x_ref, off_ref, grp_ref, noise_ref,
    table_ref, cos_ref, sin_ref, small_sems, x_sems
):
    rows = x_ref.shape[0]
    small = [
        pltpu.make_async_copy(source, target, small_sems.at[i])
        for i, (source, target) in enumerate(
            ((off_hbm, off_ref), (grp_hbm, grp_ref), (noise_hbm, noise_ref), (table_hbm, table_ref))
        )
    ]
    for copy in small:
        copy.start()
    parts = []
    step = rows // PARTS
    for g in range(PARTS):
        part = slice(g * step, (g + 1) * step)
        copy = pltpu.make_async_copy(x_hbm.at[part, :], x_ref.at[part, :], x_sems.at[g])
        copy.start()
        parts.append(copy)
    out_lane = lax.broadcasted_iota(jnp.int32, (LANES, LANES), 1)
    in_lane = lax.broadcasted_iota(jnp.int32, (LANES, LANES), 0)
    is_real = (out_lane // CYCLES) % 2 == 0
    swap = jnp.where(
        is_real,
        jnp.where(in_lane == out_lane + CYCLES, -1.0, 0.0),
        jnp.where(in_lane == out_lane - CYCLES, 1.0, 0.0),
    ).astype(BF16)
    for copy in small:
        copy.wait()
    noise = jnp.concatenate([noise_ref[...]] * (LANES // CYCLES), axis=1)

    def down(row):
        return jnp.broadcast_to(row.astype(F32), (LANES, rows)).T

    defocus = 10000.0 + 1500.0 * down(grp_ref[...])
    chi_cos, chi_sin = turn_trig(defocus * table_ref[2 * HALF : 2 * HALF + 1, :])
    ctf = -(0.995 * chi_sin + 0.1 * chi_cos) * table_ref[2 * HALF + 1 : 2 * HALF + 2, :]
    scale = ctf / noise
    power_ref[...] = ctf * scale
    shift_x = down(off_ref[0:1, :])
    shift_y = down(off_ref[1:2, :])

    def phases(t):
        turns = shift_x * table_ref[t : t + 1, :] + shift_y * table_ref[HALF + t : HALF + t + 1, :]
        cosine, sine = turn_trig(turns)
        return cosine * scale, sine * scale

    for t in range(AHEAD):
        cos_ref[t], sin_ref[t] = phases(t)
    for copy in parts:
        copy.wait()
    for t in range(HALF):
        cosine, sine = (cos_ref[t], sin_ref[t]) if t < AHEAD else phases(t)
        for tile, sign in ((t, 1), (t + HALF, -1)):
            x = x_ref[:, tile * LANES : (tile + 1) * LANES]
            other = jnp.dot(x, swap, preferred_element_type=F32)
            first = x.astype(F32) * cosine
            second = other * sine
            out = first + second if sign > 0 else first - second
            adj_ref[:, tile * LANES : (tile + 1) * LANES] = out.astype(BF16)
            turned_ref[tile * LANES : (tile + 1) * LANES, :] = out.T.astype(BF16)


def score(held, got_ref, turned_ref, power_ref, prior_ref, e_ref, best_ref, lse_ref, wide):
    classes = prior_ref.shape[1]
    particles = turned_ref.shape[1]
    row = lax.broadcasted_iota(jnp.int32, (classes, classes), 0)
    place = jnp.zeros((classes, classes), jnp.int32)
    for i, c in enumerate(held):
        place = jnp.where(row == i, c, place)
    diagonal = place == lax.broadcasted_iota(jnp.int32, (classes, classes), 1)
    prior = jnp.sum(jnp.where(diagonal, jnp.broadcast_to(prior_ref[...], (classes, classes)), 0.0), axis=1, keepdims=True)
    wide[...] = got_ref[...].astype(F32)
    blocks = []
    ref_power = jnp.zeros((classes, LANES), F32)
    for j in range(ROT):
        block = wide[pl.ds(j, classes, stride=CHUNK), :]
        ref_power = ref_power + block * block
        blocks.append(block.astype(BF16))
    energy = 0.5 * lax.dot_general(
        ref_power, power_ref[...], (((1,), (1,)), ((), ())), precision=HIGHEST, preferred_element_type=F32
    )
    bias = prior - energy
    bias = jnp.concatenate([bias, bias], axis=1)
    lhs = jnp.concatenate(
        [jnp.concatenate([blocks[(i + 2 * r) % ROT] for i in range(ROT)], axis=1) for r in range(HALF)], axis=0
    )
    tiles = [turned_ref[i * LANES : (i + 1) * LANES, :] for i in range(ROT)]
    rhs = jnp.concatenate([jnp.concatenate([tiles[i], tiles[i - 1]], axis=1) for i in range(ROT)], axis=0)
    raw = jnp.dot(lhs, rhs, preferred_element_type=F32).reshape(HALF, classes, 2 * particles)
    scores = raw + bias[None]
    best = jnp.max(jnp.max(scores, axis=0), axis=0, keepdims=True)
    best = jnp.maximum(best[:, :particles], best[:, particles:])
    both = jnp.concatenate([best, best], axis=1)
    e = jnp.exp(scores - both[None])
    total = jnp.sum(jnp.sum(e, axis=0), axis=0, keepdims=True)
    total = total[:, :particles] + total[:, particles:]
    e_ref[...] = e.reshape(HALF * classes, 2 * particles)
    best_ref[...] = best
    lse_ref[...] = best + jnp.log(total)


def first_score_kernel(held, alone, *refs):
    *rest, lse_ref, _ = refs
    here = True if alone else lax.axis_index("cls") == 1

    @pl.when(here)
    def _():
        score(held, *refs)

    @pl.when(jnp.logical_not(here))
    def _():
        lse_ref[...] = jnp.zeros_like(lse_ref)


def second_score_kernel(held, *refs):
    sources, before, after, wide = refs[:4], refs[4:7], refs[7:10], refs[10]
    here = lax.axis_index("cls") == 0

    @pl.when(here)
    def _():
        score(held, *sources, *after, wide)

    @pl.when(jnp.logical_not(here))
    def _():
        for source, target in zip(before, after):
            target[...] = source[...]


def total_evidence(lse_refs):
    lse = jnp.concatenate([ref[...] for ref in lse_refs], axis=0)
    top = jnp.max(lse, axis=0, keepdims=True)
    return top + jnp.log(jnp.sum(jnp.exp(lse - top), axis=0, keepdims=True))


def sums(e_ref, best_ref, adj_ref, power_ref, *rest):
    *lse_refs, out_ref, wide = rest
    particles = adj_ref.shape[0]
    classes = e_ref.shape[0] // HALF
    factor = jnp.exp(best_ref[...] - total_evidence(lse_refs))
    post = e_ref[...] * jnp.concatenate([factor, factor], axis=1)
    mass = jnp.sum(post.reshape(HALF, classes, 2 * particles), axis=0)
    mass = mass[:, :particles] + mass[:, particles:]
    weight = jnp.dot(mass, power_ref[...], precision=HIGHEST, preferred_element_type=F32)
    post = post.astype(BF16)
    blocks = [
        post[(q // 2) * classes : (q // 2 + 1) * classes, (q % 2) * particles : (q % 2 + 1) * particles]
        for q in range(ROT)
    ]
    lhs = jnp.concatenate(
        [jnp.concatenate([blocks[(2 * r - i) % ROT] for i in range(ROT)], axis=1) for r in range(HALF)], axis=0
    )
    tiles = [adj_ref[:, i * LANES : (i + 1) * LANES] for i in range(ROT)]
    rhs = jnp.concatenate(
        [jnp.concatenate([tiles[i], tiles[(i + 1) % ROT]], axis=1) for i in range(ROT)], axis=0
    )
    data = jnp.dot(lhs, rhs, preferred_element_type=F32)
    for n in range(ROT):
        r, d = n // 2, n % 2
        wide[pl.ds(n, classes, stride=CHUNK), :] = data[r * classes : (r + 1) * classes, d * LANES : (d + 1) * LANES]
    group = lax.broadcasted_iota(jnp.int32, weight.shape, 1) // CYCLES
    high = weight.astype(BF16).astype(F32)
    rest = weight - high
    middle = rest.astype(BF16).astype(F32)
    terms = jnp.where(group == 0, high, jnp.where(group == 1, middle, jnp.where(group == 2, rest - middle, 0.0)))
    wide[pl.ds(ROT, classes, stride=CHUNK), :] = terms
    for n in range(ROT + 1, CHUNK):
        wide[pl.ds(n, classes, stride=CHUNK), :] = jnp.zeros((classes, LANES), F32)
    out_ref[...] = wide[...].astype(BF16)


def first_sum_kernel(alone, *refs):
    @pl.when(True if alone else lax.axis_index("cls") == 0)
    def _():
        sums(*refs)


def second_sum_kernel(*refs):
    *sources, before, out_ref, wide = refs
    here = lax.axis_index("cls") == 1

    @pl.when(here)
    def _():
        sums(*sources, out_ref, wide)

    @pl.when(jnp.logical_not(here))
    def _():
        out_ref[...] = before[...]


def final_kernel(senders, got_ref, *rest):
    *lse_refs, data_ref, weight_ref, evidence_ref = rest
    evidence_ref[...] = total_evidence(lse_refs)
    owned = data_ref.shape[0]
    got = got_ref[...].astype(F32).reshape(senders, owned * CHUNK, LANES)
    total = jnp.sum(got, axis=0)
    for o in range(owned):
        base = o * CHUNK
        for n in range(ROT):
            data_ref[o : o + 1, n * LANES : (n + 1) * LANES] = total[base + n : base + n + 1, :]
        terms = total[base + ROT : base + ROT + 1, :]
        weight_ref[o : o + 1, :] = (
            terms[:, :CYCLES] + terms[:, CYCLES : 2 * CYCLES] + terms[:, 2 * CYCLES : 3 * CYCLES]
        )


def call(kernel, outs, scratch=(), in_hbm=(), out_space=pltpu.VMEM, flops=0, bytes_accessed=0):
    def run(*args):
        args = [pltpu.with_memory_space_constraint(x, pltpu.HBM) if i in in_hbm else x for i, x in enumerate(args)]
        return pl.pallas_call(
            kernel,
            out_shape=tuple(jax.ShapeDtypeStruct(shape, dtype) for shape, dtype in outs),
            in_specs=[pl.BlockSpec(memory_space=pltpu.HBM if i in in_hbm else pltpu.VMEM) for i in range(len(args))],
            out_specs=tuple(pl.BlockSpec(memory_space=out_space) for _ in outs),
            scratch_shapes=list(scratch),
            compiler_params=pltpu.CompilerParams(vmem_limit_bytes=VMEM_LIMIT),
            cost_estimate=pl.CostEstimate(flops=flops, bytes_accessed=bytes_accessed, transcendentals=0),
        )(*args)

    return run


def exchange_order(dom_size):
    if dom_size == len(ORDER):
        return ORDER
    root = dom_size * 3 // 4 - 1
    return [(i + root) % dom_size for i in range(dom_size)]


def per_device(particles, references, log_prior, noise_var, offsets, groups):
    dom_size = lax.axis_size("dom")
    cls_size = lax.axis_size("cls")
    rows, samples = particles.shape
    owned = references.shape[0]
    classes = log_prior.shape[0]
    message = classes * CHUNK
    table = lane_tables()

    order = exchange_order(dom_size)
    exchange = functools.partial(
        lax.all_to_all,
        axis_name="dom",
        split_axis=0,
        concat_axis=0,
        axis_index_groups=[order],
        tiled=True,
    )
    (own,) = call(
        retile_kernel,
        [((owned * CHUNK, LANES), BF16)],
        [pltpu.VMEM((owned * CHUNK, LANES), F32)],
        bytes_accessed=message * LANES * 2,
    )(references)
    spread = jnp.broadcast_to(own[None], (dom_size, owned * CHUNK, LANES)).reshape(message, LANES)
    got = exchange(spread)
    adjusted, turned, power = call(
        prepare_kernel,
        [((rows, samples), BF16), ((samples, rows), BF16), ((rows, LANES), F32)],
        [
            pltpu.VMEM((rows, samples), BF16),
            pltpu.VMEM((2, rows), jnp.int32),
            pltpu.VMEM((1, rows), jnp.int32),
            pltpu.VMEM((1, CYCLES), F32),
            pltpu.VMEM(table.shape, F32),
            pltpu.VMEM((AHEAD, rows, LANES), F32),
            pltpu.VMEM((AHEAD, rows, LANES), F32),
            pltpu.SemaphoreType.DMA((4,)),
            pltpu.SemaphoreType.DMA((PARTS,)),
        ],
        in_hbm=range(5),
        flops=rows * samples * 300,
        bytes_accessed=rows * samples * 6,
    )(particles, offsets.T, groups.reshape(1, rows), noise_var.reshape(1, CYCLES), jnp.asarray(table))
    dot_flops = 2 * ROT * classes * rows * samples
    held = [d * owned + o for d in order for o in range(owned)]
    prior = log_prior.reshape(1, classes)
    scored = [((HALF * classes, 2 * rows), F32), ((1, rows), F32), ((1, rows), F32)]
    wide = [pltpu.VMEM((message, LANES), F32)]
    costs = dict(flops=dot_flops, bytes_accessed=rows * samples * 4)
    summed = [((message, LANES), BF16)]
    two = cls_size == 2
    e, best, lse = call(functools.partial(first_score_kernel, held, not two), scored, wide, **costs)(
        got, turned, power, prior
    )
    if two:
        early = lax.ppermute(lse, "cls", [(0, 1), (1, 0)])
        e, best, lse = call(functools.partial(second_score_kernel, held), scored, wide, **costs)(
            got, turned, power, prior, e, best, lse
        )
        all_lse = (lse, lax.ppermute(lse, "cls", [(0, 1), (1, 0)]))
        (part,) = call(functools.partial(first_sum_kernel, False), summed, wide, **costs)(
            e, best, adjusted, power, lse, early
        )
        (partial_sums,) = call(second_sum_kernel, summed, wide, **costs)(e, best, adjusted, power, *all_lse, part)
    else:
        all_lse = (lax.all_gather(lse, "cls", axis=0, tiled=True),)
        (partial_sums,) = call(functools.partial(first_sum_kernel, True), summed, wide, **costs)(
            e, best, adjusted, power, *all_lse
        )
    mine = exchange(partial_sums)
    data, weight, evidence = call(
        functools.partial(final_kernel, dom_size),
        [((owned, samples), F32), ((owned, CYCLES), F32), ((1, rows), F32)],
        bytes_accessed=message * LANES * 2,
    )(mine, *all_lse)
    return data, weight, evidence.reshape(rows)


def solution(mesh):
    return jax.shard_map(
        per_device,
        mesh=mesh,
        in_specs=(P("dom", None), P(("cls", "dom"), None), P("cls"), P(), P("dom", None), P("dom")),
        out_specs=(P(("cls", "dom"), None), P(("cls", "dom"), None), P("dom")),
        check_vma=False,
    )
```

```python
import functools
import math

import jax
import jax.numpy as jnp
import numpy as np
from jax import lax
from jax.experimental import pallas as pl
from jax.experimental.pallas import tpu as pltpu
from jax.sharding import PartitionSpec as P

BOX = 64
CYCLES = 32
ROT = 36
ANGLES = 72
LANES = 128
HALF = ROT // 2
PARTS = 4
DEPTH = 4
AHEAD = 6
CHUNK = 40
ORDER = [11, 10, 0, 5, 6, 4, 14, 1, 15, 8, 13, 7, 3, 2, 12, 9]
F32 = jnp.float32
BF16 = jnp.bfloat16
HIGHEST = lax.Precision.HIGHEST
VMEM_LIMIT = 24 * 1024 * 1024


def trig_polynomials():
    nodes = 0.125 + 0.125 * np.cos(np.pi * (np.arange(400) + 0.5) / 400)
    root = np.sqrt(nodes)
    fits = []
    for values, degree in ((np.cos(2 * np.pi * root), 6), (np.sin(2 * np.pi * root) / root, 5)):
        fit = np.polynomial.Chebyshev.fit(nodes, values, degree, domain=[0, 0.25])
        fits.append([float(c) for c in fit.convert(kind=np.polynomial.Polynomial).coef])
    return fits


COS_COEF, SIN_COEF = trig_polynomials()


def horner(coef, x):
    total = coef[-1] * x + coef[-2]
    for c in coef[-3::-1]:
        total = total * x + c
    return total


def turn_trig(turns):
    r = turns - jnp.floor(turns + 0.5)
    square = r * r
    return horner(COS_COEF, square), horner(SIN_COEF, square) * r


def lane_tables():
    lane = np.arange(LANES)
    cycle = lane % CYCLES
    rows = []
    for component in (np.cos, np.sin):
        for t in range(HALF):
            theta = 2.0 * np.pi * (2 * t + lane // 64) / ANGLES
            rows.append((cycle + 1.0) * component(theta) / BOX)
    square = ((cycle + 1.0) / (1.5 * BOX)) ** 2
    rows.append(0.0197 / 2.0 * square)
    rows.append(np.exp(-10.0 * square))
    rows += [np.zeros(LANES)] * (-len(rows) % 8)
    return np.stack(rows).astype(np.float32)


def retile_kernel(ref_ref, out_ref, rows):
    owned, depth, width = out_ref.shape
    for o in range(owned):
        row = ref_ref[o : o + 1, :].astype(F32)
        for a in range(depth):
            rows[a : a + 1, :] = row[:, a * width : (a + 1) * width]
        out_ref[o] = rows[...].astype(BF16)


def prepare_kernel(
    x_hbm, off_hbm, grp_hbm, noise_hbm, table_hbm, adj_ref, turned_ref, power_ref, x_ref, off_ref, grp_ref, noise_ref,
    table_ref, cos_ref, sin_ref, small_sems, x_sems
):
    rows = x_ref.shape[0]
    small = [
        pltpu.make_async_copy(source, target, small_sems.at[i])
        for i, (source, target) in enumerate(
            ((off_hbm, off_ref), (grp_hbm, grp_ref), (noise_hbm, noise_ref), (table_hbm, table_ref))
        )
    ]
    for copy in small:
        copy.start()
    parts = []
    step = rows // PARTS
    for g in range(PARTS):
        part = slice(g * step, (g + 1) * step)
        copy = pltpu.make_async_copy(x_hbm.at[part, :], x_ref.at[part, :], x_sems.at[g])
        copy.start()
        parts.append(copy)
    out_lane = lax.broadcasted_iota(jnp.int32, (LANES, LANES), 1)
    in_lane = lax.broadcasted_iota(jnp.int32, (LANES, LANES), 0)
    is_real = (out_lane // CYCLES) % 2 == 0
    swap = jnp.where(
        is_real,
        jnp.where(in_lane == out_lane + CYCLES, -1.0, 0.0),
        jnp.where(in_lane == out_lane - CYCLES, 1.0, 0.0),
    ).astype(BF16)
    for copy in small:
        copy.wait()
    noise = jnp.concatenate([noise_ref[...]] * (LANES // CYCLES), axis=1)

    def down(row):
        return jnp.broadcast_to(row.astype(F32), (LANES, rows)).T

    defocus = 10000.0 + 1500.0 * down(grp_ref[...])
    chi_cos, chi_sin = turn_trig(defocus * table_ref[2 * HALF : 2 * HALF + 1, :])
    ctf = -(0.995 * chi_sin + 0.1 * chi_cos) * table_ref[2 * HALF + 1 : 2 * HALF + 2, :]
    scale = ctf / noise
    power_ref[...] = ctf * scale
    shift_x = down(off_ref[0:1, :])
    shift_y = down(off_ref[1:2, :])

    def phases(t):
        turns = shift_x * table_ref[t : t + 1, :] + shift_y * table_ref[HALF + t : HALF + t + 1, :]
        cosine, sine = turn_trig(turns)
        return cosine * scale, sine * scale

    for t in range(AHEAD):
        cos_ref[t], sin_ref[t] = phases(t)
    for copy in parts:
        copy.wait()
    for t in range(HALF):
        cosine, sine = (cos_ref[t], sin_ref[t]) if t < AHEAD else phases(t)
        for tile, sign in ((t, 1), (t + HALF, -1)):
            x = x_ref[:, tile * LANES : (tile + 1) * LANES]
            other = jnp.dot(x, swap, preferred_element_type=F32)
            first = x.astype(F32) * cosine
            second = other * sine
            out = first + second if sign > 0 else first - second
            adj_ref[:, tile * LANES : (tile + 1) * LANES] = out.astype(BF16)
            turned_ref[tile * LANES : (tile + 1) * LANES, :] = out.T.astype(BF16)


def score(held, got_ref, turned_ref, power_ref, prior_ref, e_ref, best_ref, lse_ref, wide):
    classes = prior_ref.shape[1]
    particles = turned_ref.shape[1]
    row = lax.broadcasted_iota(jnp.int32, (classes, classes), 0)
    place = jnp.zeros((classes, classes), jnp.int32)
    for i, c in enumerate(held):
        place = jnp.where(row == i, c, place)
    diagonal = place == lax.broadcasted_iota(jnp.int32, (classes, classes), 1)
    prior = jnp.sum(jnp.where(diagonal, jnp.broadcast_to(prior_ref[...], (classes, classes)), 0.0), axis=1, keepdims=True)
    depth, width = got_ref.shape[1:]
    across = width // LANES
    for i in range(classes):
        message = got_ref[i].astype(F32)
        for b in range(across):
            at = (b * classes + i) * depth
            wide[at : at + depth, :] = message[:, b * LANES : (b + 1) * LANES]
    blocks = []
    ref_power = jnp.zeros((classes, LANES), F32)
    for j in range(ROT):
        block = wide[pl.ds(j % across * classes * depth + j // across, classes, stride=depth), :]
        ref_power = ref_power + block * block
        blocks.append(block.astype(BF16))
    energy = 0.5 * lax.dot_general(
        ref_power, power_ref[...], (((1,), (1,)), ((), ())), precision=HIGHEST, preferred_element_type=F32
    )
    bias = prior - energy
    bias = jnp.concatenate([bias, bias], axis=1)
    lhs = jnp.concatenate(
        [jnp.concatenate([blocks[(i + 2 * r) % ROT] for i in range(ROT)], axis=1) for r in range(HALF)], axis=0
    )
    tiles = [turned_ref[i * LANES : (i + 1) * LANES, :] for i in range(ROT)]
    rhs = jnp.concatenate([jnp.concatenate([tiles[i], tiles[i - 1]], axis=1) for i in range(ROT)], axis=0)
    raw = jnp.dot(lhs, rhs, preferred_element_type=F32).reshape(HALF, classes, 2 * particles)
    scores = raw + bias[None]
    best = jnp.max(jnp.max(scores, axis=0), axis=0, keepdims=True)
    best = jnp.maximum(best[:, :particles], best[:, particles:])
    both = jnp.concatenate([best, best], axis=1)
    e = jnp.exp(scores - both[None])
    total = jnp.sum(jnp.sum(e, axis=0), axis=0, keepdims=True)
    total = total[:, :particles] + total[:, particles:]
    e_ref[...] = e.reshape(HALF * classes, 2 * particles)
    best_ref[...] = best
    lse_ref[...] = best + jnp.log(total)


def first_score_kernel(held, alone, *refs):
    *rest, lse_ref, _ = refs
    here = True if alone else lax.axis_index("cls") == 1

    @pl.when(here)
    def _():
        score(held, *refs)

    @pl.when(jnp.logical_not(here))
    def _():
        lse_ref[...] = jnp.zeros_like(lse_ref)


def second_score_kernel(held, *refs):
    sources, before, after, wide = refs[:4], refs[4:7], refs[7:10], refs[10]
    here = lax.axis_index("cls") == 0

    @pl.when(here)
    def _():
        score(held, *sources, *after, wide)

    @pl.when(jnp.logical_not(here))
    def _():
        for source, target in zip(before, after):
            target[...] = source[...]


def total_evidence(lse_refs):
    lse = jnp.concatenate([ref[...] for ref in lse_refs], axis=0)
    top = jnp.max(lse, axis=0, keepdims=True)
    return top + jnp.log(jnp.sum(jnp.exp(lse - top), axis=0, keepdims=True))


def sums(e_ref, best_ref, adj_ref, power_ref, *rest):
    *lse_refs, out_ref, wide = rest
    particles = adj_ref.shape[0]
    classes = e_ref.shape[0] // HALF
    factor = jnp.exp(best_ref[...] - total_evidence(lse_refs))
    post = e_ref[...] * jnp.concatenate([factor, factor], axis=1)
    mass = jnp.sum(post.reshape(HALF, classes, 2 * particles), axis=0)
    mass = mass[:, :particles] + mass[:, particles:]
    weight = jnp.dot(mass, power_ref[...], precision=HIGHEST, preferred_element_type=F32)
    post = post.astype(BF16)
    blocks = [
        post[(q // 2) * classes : (q // 2 + 1) * classes, (q % 2) * particles : (q % 2 + 1) * particles]
        for q in range(ROT)
    ]
    lhs = jnp.concatenate(
        [jnp.concatenate([blocks[(2 * r - i) % ROT] for i in range(ROT)], axis=1) for r in range(HALF)], axis=0
    )
    tiles = [adj_ref[:, i * LANES : (i + 1) * LANES] for i in range(ROT)]
    rhs = jnp.concatenate(
        [jnp.concatenate([tiles[i], tiles[(i + 1) % ROT]], axis=1) for i in range(ROT)], axis=0
    )
    data = jnp.dot(lhs, rhs, preferred_element_type=F32)
    for n in range(ROT):
        r, d = n // 2, n % 2
        wide[pl.ds(n, classes, stride=CHUNK), :] = data[r * classes : (r + 1) * classes, d * LANES : (d + 1) * LANES]
    group = lax.broadcasted_iota(jnp.int32, weight.shape, 1) // CYCLES
    high = weight.astype(BF16).astype(F32)
    rest = weight - high
    middle = rest.astype(BF16).astype(F32)
    terms = jnp.where(group == 0, high, jnp.where(group == 1, middle, jnp.where(group == 2, rest - middle, 0.0)))
    wide[pl.ds(ROT, classes, stride=CHUNK), :] = terms
    for n in range(ROT + 1, CHUNK):
        wide[pl.ds(n, classes, stride=CHUNK), :] = jnp.zeros((classes, LANES), F32)
    out_ref[...] = wide[...].astype(BF16)


def first_sum_kernel(alone, *refs):
    @pl.when(True if alone else lax.axis_index("cls") == 0)
    def _():
        sums(*refs)


def second_sum_kernel(*refs):
    *sources, before, out_ref, wide = refs
    here = lax.axis_index("cls") == 1

    @pl.when(here)
    def _():
        sums(*sources, out_ref, wide)

    @pl.when(jnp.logical_not(here))
    def _():
        out_ref[...] = before[...]


def final_kernel(senders, got_ref, *rest):
    *lse_refs, data_ref, weight_ref, evidence_ref = rest
    evidence_ref[...] = total_evidence(lse_refs)
    owned = data_ref.shape[0]
    got = got_ref[...].astype(F32).reshape(senders, owned * CHUNK, LANES)
    total = jnp.sum(got, axis=0)
    for o in range(owned):
        base = o * CHUNK
        for n in range(ROT):
            data_ref[o : o + 1, n * LANES : (n + 1) * LANES] = total[base + n : base + n + 1, :]
        terms = total[base + ROT : base + ROT + 1, :]
        weight_ref[o : o + 1, :] = (
            terms[:, :CYCLES] + terms[:, CYCLES : 2 * CYCLES] + terms[:, 2 * CYCLES : 3 * CYCLES]
        )


def call(kernel, outs, scratch=(), in_hbm=(), out_space=pltpu.VMEM, flops=0, bytes_accessed=0):
    def run(*args):
        args = [pltpu.with_memory_space_constraint(x, pltpu.HBM) if i in in_hbm else x for i, x in enumerate(args)]
        return pl.pallas_call(
            kernel,
            out_shape=tuple(jax.ShapeDtypeStruct(shape, dtype) for shape, dtype in outs),
            in_specs=[pl.BlockSpec(memory_space=pltpu.HBM if i in in_hbm else pltpu.VMEM) for i in range(len(args))],
            out_specs=tuple(pl.BlockSpec(memory_space=out_space) for _ in outs),
            scratch_shapes=list(scratch),
            compiler_params=pltpu.CompilerParams(vmem_limit_bytes=VMEM_LIMIT),
            cost_estimate=pl.CostEstimate(flops=flops, bytes_accessed=bytes_accessed, transcendentals=0),
        )(*args)

    return run


def exchange_order(dom_size):
    if dom_size == len(ORDER):
        return ORDER
    root = dom_size * 3 // 4 - 1
    return [(i + root) % dom_size for i in range(dom_size)]


def per_device(particles, references, log_prior, noise_var, offsets, groups):
    dom_size = lax.axis_size("dom")
    cls_size = lax.axis_size("cls")
    rows, samples = particles.shape
    owned = references.shape[0]
    classes = log_prior.shape[0]
    message = classes * CHUNK
    table = lane_tables()

    order = exchange_order(dom_size)
    exchange = functools.partial(
        lax.all_to_all,
        axis_name="dom",
        split_axis=0,
        concat_axis=0,
        axis_index_groups=[order],
        tiled=True,
    )
    width = samples // DEPTH
    (own,) = call(
        retile_kernel,
        [((owned, DEPTH, width), BF16)],
        [pltpu.VMEM((DEPTH, width), F32)],
        bytes_accessed=owned * samples * 4,
    )(references)
    spread = jnp.broadcast_to(own[None], (dom_size, owned, DEPTH, width)).reshape(classes, DEPTH, width)
    got = exchange(spread)
    adjusted, turned, power = call(
        prepare_kernel,
        [((rows, samples), BF16), ((samples, rows), BF16), ((rows, LANES), F32)],
        [
            pltpu.VMEM((rows, samples), BF16),
            pltpu.VMEM((2, rows), jnp.int32),
            pltpu.VMEM((1, rows), jnp.int32),
            pltpu.VMEM((1, CYCLES), F32),
            pltpu.VMEM(table.shape, F32),
            pltpu.VMEM((AHEAD, rows, LANES), F32),
            pltpu.VMEM((AHEAD, rows, LANES), F32),
            pltpu.SemaphoreType.DMA((4,)),
            pltpu.SemaphoreType.DMA((PARTS,)),
        ],
        in_hbm=range(5),
        flops=rows * samples * 300,
        bytes_accessed=rows * samples * 6,
    )(particles, offsets.T, groups.reshape(1, rows), noise_var.reshape(1, CYCLES), jnp.asarray(table))
    dot_flops = 2 * ROT * classes * rows * samples
    held = [d * owned + o for d in order for o in range(owned)]
    prior = log_prior.reshape(1, classes)
    scored = [((HALF * classes, 2 * rows), F32), ((1, rows), F32), ((1, rows), F32)]
    spots = [pltpu.VMEM((classes * samples // LANES, LANES), F32)]
    wide = [pltpu.VMEM((message, LANES), F32)]
    costs = dict(flops=dot_flops, bytes_accessed=rows * samples * 4)
    summed = [((message, LANES), BF16)]
    two = cls_size == 2
    e, best, lse = call(functools.partial(first_score_kernel, held, not two), scored, spots, **costs)(
        got, turned, power, prior
    )
    if two:
        early = lax.ppermute(lse, "cls", [(0, 1), (1, 0)])
        e, best, lse = call(functools.partial(second_score_kernel, held), scored, spots, **costs)(
            got, turned, power, prior, e, best, lse
        )
        all_lse = (lse, lax.ppermute(lse, "cls", [(0, 1), (1, 0)]))
        (part,) = call(functools.partial(first_sum_kernel, False), summed, wide, **costs)(
            e, best, adjusted, power, lse, early
        )
        (partial_sums,) = call(second_sum_kernel, summed, wide, **costs)(e, best, adjusted, power, *all_lse, part)
    else:
        all_lse = (lax.all_gather(lse, "cls", axis=0, tiled=True),)
        (partial_sums,) = call(functools.partial(first_sum_kernel, True), summed, wide, **costs)(
            e, best, adjusted, power, *all_lse
        )
    mine = exchange(partial_sums)
    data, weight, evidence = call(
        functools.partial(final_kernel, dom_size),
        [((owned, samples), F32), ((owned, CYCLES), F32), ((1, rows), F32)],
        bytes_accessed=message * LANES * 2,
    )(mine, *all_lse)
    return data, weight, evidence.reshape(rows)


def solution(mesh):
    return jax.shard_map(
        per_device,
        mesh=mesh,
        in_specs=(P("dom", None), P(("cls", "dom"), None), P("cls"), P(), P("dom", None), P("dom")),
        out_specs=(P(("cls", "dom"), None), P(("cls", "dom"), None), P("dom")),
        check_vma=False,
    )
```

```python
import functools
import math

import jax
import jax.numpy as jnp
import numpy as np
from jax import lax
from jax.experimental import pallas as pl
from jax.experimental.pallas import tpu as pltpu
from jax.sharding import PartitionSpec as P

BOX = 64
CYCLES = 32
ROT = 36
ANGLES = 72
LANES = 128
HALF = ROT // 2
PARTS = 4
DEPTH = 4
AHEAD = 6
ACROSS = 19
ORDER = [11, 10, 0, 5, 6, 4, 14, 1, 15, 8, 13, 7, 3, 2, 12, 9]
F32 = jnp.float32
BF16 = jnp.bfloat16
HIGHEST = lax.Precision.HIGHEST
VMEM_LIMIT = 24 * 1024 * 1024


def trig_polynomials():
    nodes = 0.125 + 0.125 * np.cos(np.pi * (np.arange(400) + 0.5) / 400)
    root = np.sqrt(nodes)
    fits = []
    for values, degree in ((np.cos(2 * np.pi * root), 6), (np.sin(2 * np.pi * root) / root, 5)):
        fit = np.polynomial.Chebyshev.fit(nodes, values, degree, domain=[0, 0.25])
        fits.append([float(c) for c in fit.convert(kind=np.polynomial.Polynomial).coef])
    return fits


COS_COEF, SIN_COEF = trig_polynomials()


def horner(coef, x):
    total = coef[-1] * x + coef[-2]
    for c in coef[-3::-1]:
        total = total * x + c
    return total


def turn_trig(turns):
    r = turns - jnp.floor(turns + 0.5)
    square = r * r
    return horner(COS_COEF, square), horner(SIN_COEF, square) * r


def lane_tables():
    lane = np.arange(LANES)
    cycle = lane % CYCLES
    rows = []
    for component in (np.cos, np.sin):
        for t in range(HALF):
            theta = 2.0 * np.pi * (2 * t + lane // 64) / ANGLES
            rows.append((cycle + 1.0) * component(theta) / BOX)
    square = ((cycle + 1.0) / (1.5 * BOX)) ** 2
    rows.append(0.0197 / 2.0 * square)
    rows.append(np.exp(-10.0 * square))
    rows += [np.zeros(LANES)] * (-len(rows) % 8)
    return np.stack(rows).astype(np.float32)


def retile_kernel(ref_ref, out_ref, rows):
    owned, depth, width = out_ref.shape
    for o in range(owned):
        row = ref_ref[o : o + 1, :].astype(F32)
        for a in range(depth):
            rows[a : a + 1, :] = row[:, a * width : (a + 1) * width]
        out_ref[o] = rows[...].astype(BF16)


def prepare_kernel(
    x_hbm, off_hbm, grp_hbm, noise_hbm, table_hbm, adj_ref, turned_ref, power_ref, x_ref, off_ref, grp_ref, noise_ref,
    table_ref, cos_ref, sin_ref, small_sems, x_sems
):
    rows = x_ref.shape[0]
    small = [
        pltpu.make_async_copy(source, target, small_sems.at[i])
        for i, (source, target) in enumerate(
            ((off_hbm, off_ref), (grp_hbm, grp_ref), (noise_hbm, noise_ref), (table_hbm, table_ref))
        )
    ]
    for copy in small:
        copy.start()
    parts = []
    step = rows // PARTS
    for g in range(PARTS):
        part = slice(g * step, (g + 1) * step)
        copy = pltpu.make_async_copy(x_hbm.at[part, :], x_ref.at[part, :], x_sems.at[g])
        copy.start()
        parts.append(copy)
    out_lane = lax.broadcasted_iota(jnp.int32, (LANES, LANES), 1)
    in_lane = lax.broadcasted_iota(jnp.int32, (LANES, LANES), 0)
    is_real = (out_lane // CYCLES) % 2 == 0
    swap = jnp.where(
        is_real,
        jnp.where(in_lane == out_lane + CYCLES, -1.0, 0.0),
        jnp.where(in_lane == out_lane - CYCLES, 1.0, 0.0),
    ).astype(BF16)
    for copy in small:
        copy.wait()
    noise = jnp.concatenate([noise_ref[...]] * (LANES // CYCLES), axis=1)

    def down(row):
        return jnp.broadcast_to(row.astype(F32), (LANES, rows)).T

    defocus = 10000.0 + 1500.0 * down(grp_ref[...])
    chi_cos, chi_sin = turn_trig(defocus * table_ref[2 * HALF : 2 * HALF + 1, :])
    ctf = -(0.995 * chi_sin + 0.1 * chi_cos) * table_ref[2 * HALF + 1 : 2 * HALF + 2, :]
    scale = ctf / noise
    power_ref[...] = ctf * scale
    shift_x = down(off_ref[0:1, :])
    shift_y = down(off_ref[1:2, :])

    def phases(t):
        turns = shift_x * table_ref[t : t + 1, :] + shift_y * table_ref[HALF + t : HALF + t + 1, :]
        cosine, sine = turn_trig(turns)
        return cosine * scale, sine * scale

    for t in range(AHEAD):
        cos_ref[t], sin_ref[t] = phases(t)
    for copy in parts:
        copy.wait()
    for t in range(HALF):
        cosine, sine = (cos_ref[t], sin_ref[t]) if t < AHEAD else phases(t)
        for tile, sign in ((t, 1), (t + HALF, -1)):
            x = x_ref[:, tile * LANES : (tile + 1) * LANES]
            other = jnp.dot(x, swap, preferred_element_type=F32)
            first = x.astype(F32) * cosine
            second = other * sine
            out = first + second if sign > 0 else first - second
            adj_ref[:, tile * LANES : (tile + 1) * LANES] = out.astype(BF16)
            turned_ref[tile * LANES : (tile + 1) * LANES, :] = out.T.astype(BF16)


def score(held, got_ref, turned_ref, power_ref, prior_ref, e_ref, best_ref, lse_ref, wide):
    classes = prior_ref.shape[1]
    particles = turned_ref.shape[1]
    row = lax.broadcasted_iota(jnp.int32, (classes, classes), 0)
    place = jnp.zeros((classes, classes), jnp.int32)
    for i, c in enumerate(held):
        place = jnp.where(row == i, c, place)
    diagonal = place == lax.broadcasted_iota(jnp.int32, (classes, classes), 1)
    prior = jnp.sum(jnp.where(diagonal, jnp.broadcast_to(prior_ref[...], (classes, classes)), 0.0), axis=1, keepdims=True)
    depth, width = got_ref.shape[1:]
    across = width // LANES
    for i in range(classes):
        message = got_ref[i].astype(F32)
        for b in range(across):
            at = (b * classes + i) * depth
            wide[at : at + depth, :] = message[:, b * LANES : (b + 1) * LANES]
    blocks = []
    ref_power = jnp.zeros((classes, LANES), F32)
    for j in range(ROT):
        block = wide[pl.ds(j % across * classes * depth + j // across, classes, stride=depth), :]
        ref_power = ref_power + block * block
        blocks.append(block.astype(BF16))
    energy = 0.5 * lax.dot_general(
        ref_power, power_ref[...], (((1,), (1,)), ((), ())), precision=HIGHEST, preferred_element_type=F32
    )
    bias = prior - energy
    bias = jnp.concatenate([bias, bias], axis=1)
    lhs = jnp.concatenate(
        [jnp.concatenate([blocks[(i + 2 * r) % ROT] for i in range(ROT)], axis=1) for r in range(HALF)], axis=0
    )
    tiles = [turned_ref[i * LANES : (i + 1) * LANES, :] for i in range(ROT)]
    rhs = jnp.concatenate([jnp.concatenate([tiles[i], tiles[i - 1]], axis=1) for i in range(ROT)], axis=0)
    raw = jnp.dot(lhs, rhs, preferred_element_type=F32).reshape(HALF, classes, 2 * particles)
    scores = raw + bias[None]
    best = jnp.max(jnp.max(scores, axis=0), axis=0, keepdims=True)
    best = jnp.maximum(best[:, :particles], best[:, particles:])
    both = jnp.concatenate([best, best], axis=1)
    e = jnp.exp(scores - both[None])
    total = jnp.sum(jnp.sum(e, axis=0), axis=0, keepdims=True)
    total = total[:, :particles] + total[:, particles:]
    e_ref[...] = e.reshape(HALF * classes, 2 * particles)
    best_ref[...] = best
    lse_ref[...] = best + jnp.log(total)


def first_score_kernel(held, alone, *refs):
    *rest, lse_ref, _ = refs
    here = True if alone else lax.axis_index("cls") == 1

    @pl.when(here)
    def _():
        score(held, *refs)

    @pl.when(jnp.logical_not(here))
    def _():
        lse_ref[...] = jnp.zeros_like(lse_ref)


def second_score_kernel(held, *refs):
    sources, before, after, wide = refs[:4], refs[4:7], refs[7:10], refs[10]
    here = lax.axis_index("cls") == 0

    @pl.when(here)
    def _():
        score(held, *sources, *after, wide)

    @pl.when(jnp.logical_not(here))
    def _():
        for source, target in zip(before, after):
            target[...] = source[...]


def total_evidence(lse_refs):
    lse = jnp.concatenate([ref[...] for ref in lse_refs], axis=0)
    top = jnp.max(lse, axis=0, keepdims=True)
    return top + jnp.log(jnp.sum(jnp.exp(lse - top), axis=0, keepdims=True))


def spot(n, classes):
    return pl.ds(n % ACROSS * classes * 2 + n // ACROSS, classes, stride=2)


def sums(e_ref, best_ref, adj_ref, power_ref, *rest):
    *lse_refs, out_ref, wide = rest
    particles = adj_ref.shape[0]
    classes = e_ref.shape[0] // HALF
    factor = jnp.exp(best_ref[...] - total_evidence(lse_refs))
    post = e_ref[...] * jnp.concatenate([factor, factor], axis=1)
    mass = jnp.sum(post.reshape(HALF, classes, 2 * particles), axis=0)
    mass = mass[:, :particles] + mass[:, particles:]
    weight = jnp.dot(mass, power_ref[...], precision=HIGHEST, preferred_element_type=F32)
    post = post.astype(BF16)
    blocks = [
        post[(q // 2) * classes : (q // 2 + 1) * classes, (q % 2) * particles : (q % 2 + 1) * particles]
        for q in range(ROT)
    ]
    lhs = jnp.concatenate(
        [jnp.concatenate([blocks[(2 * r - i) % ROT] for i in range(ROT)], axis=1) for r in range(HALF)], axis=0
    )
    tiles = [adj_ref[:, i * LANES : (i + 1) * LANES] for i in range(ROT)]
    rhs = jnp.concatenate(
        [jnp.concatenate([tiles[i], tiles[(i + 1) % ROT]], axis=1) for i in range(ROT)], axis=0
    )
    data = jnp.dot(lhs, rhs, preferred_element_type=F32)
    for n in range(ROT):
        r, d = n // 2, n % 2
        wide[spot(n, classes), :] = data[r * classes : (r + 1) * classes, d * LANES : (d + 1) * LANES]
    group = lax.broadcasted_iota(jnp.int32, weight.shape, 1) // CYCLES
    high = weight.astype(BF16).astype(F32)
    rest = weight - high
    middle = rest.astype(BF16).astype(F32)
    terms = jnp.where(group == 0, high, jnp.where(group == 1, middle, jnp.where(group == 2, rest - middle, 0.0)))
    wide[spot(ROT, classes), :] = terms
    for n in range(ROT + 1, 2 * ACROSS):
        wide[spot(n, classes), :] = jnp.zeros((classes, LANES), F32)
    for c in range(classes):
        out_ref[c] = jnp.concatenate(
            [wide[(b * classes + c) * 2 : (b * classes + c + 1) * 2, :] for b in range(ACROSS)], axis=1
        ).astype(BF16)


def first_sum_kernel(alone, *refs):
    @pl.when(True if alone else lax.axis_index("cls") == 0)
    def _():
        sums(*refs)


def second_sum_kernel(*refs):
    *sources, before, out_ref, wide = refs
    here = lax.axis_index("cls") == 1

    @pl.when(here)
    def _():
        sums(*sources, out_ref, wide)

    @pl.when(jnp.logical_not(here))
    def _():
        out_ref[...] = before[...]


def final_kernel(senders, got_ref, *rest):
    *lse_refs, data_ref, weight_ref, evidence_ref = rest
    evidence_ref[...] = total_evidence(lse_refs)
    owned = data_ref.shape[0]
    for o in range(owned):
        total = got_ref[o].astype(F32)
        for k in range(1, senders):
            total = total + got_ref[k * owned + o].astype(F32)
        blocks = [
            total[n // ACROSS : n // ACROSS + 1, n % ACROSS * LANES : (n % ACROSS + 1) * LANES] for n in range(ROT + 1)
        ]
        for n in range(ROT):
            data_ref[o : o + 1, n * LANES : (n + 1) * LANES] = blocks[n]
        terms = blocks[ROT]
        weight_ref[o : o + 1, :] = (
            terms[:, :CYCLES] + terms[:, CYCLES : 2 * CYCLES] + terms[:, 2 * CYCLES : 3 * CYCLES]
        )


def call(kernel, outs, scratch=(), in_hbm=(), out_space=pltpu.VMEM, flops=0, bytes_accessed=0):
    def run(*args):
        args = [pltpu.with_memory_space_constraint(x, pltpu.HBM) if i in in_hbm else x for i, x in enumerate(args)]
        return pl.pallas_call(
            kernel,
            out_shape=tuple(jax.ShapeDtypeStruct(shape, dtype) for shape, dtype in outs),
            in_specs=[pl.BlockSpec(memory_space=pltpu.HBM if i in in_hbm else pltpu.VMEM) for i in range(len(args))],
            out_specs=tuple(pl.BlockSpec(memory_space=out_space) for _ in outs),
            scratch_shapes=list(scratch),
            compiler_params=pltpu.CompilerParams(vmem_limit_bytes=VMEM_LIMIT),
            cost_estimate=pl.CostEstimate(flops=flops, bytes_accessed=bytes_accessed, transcendentals=0),
        )(*args)

    return run


def exchange_order(dom_size):
    if dom_size == len(ORDER):
        return ORDER
    root = dom_size * 3 // 4 - 1
    return [(i + root) % dom_size for i in range(dom_size)]


def per_device(particles, references, log_prior, noise_var, offsets, groups):
    dom_size = lax.axis_size("dom")
    cls_size = lax.axis_size("cls")
    rows, samples = particles.shape
    owned = references.shape[0]
    classes = log_prior.shape[0]
    message = classes * 2 * ACROSS
    table = lane_tables()

    order = exchange_order(dom_size)
    exchange = functools.partial(
        lax.all_to_all,
        axis_name="dom",
        split_axis=0,
        concat_axis=0,
        axis_index_groups=[order],
        tiled=True,
    )
    width = samples // DEPTH
    (own,) = call(
        retile_kernel,
        [((owned, DEPTH, width), BF16)],
        [pltpu.VMEM((DEPTH, width), F32)],
        bytes_accessed=owned * samples * 4,
    )(references)
    spread = jnp.broadcast_to(own[None], (dom_size, owned, DEPTH, width)).reshape(classes, DEPTH, width)
    got = exchange(spread)
    adjusted, turned, power = call(
        prepare_kernel,
        [((rows, samples), BF16), ((samples, rows), BF16), ((rows, LANES), F32)],
        [
            pltpu.VMEM((rows, samples), BF16),
            pltpu.VMEM((2, rows), jnp.int32),
            pltpu.VMEM((1, rows), jnp.int32),
            pltpu.VMEM((1, CYCLES), F32),
            pltpu.VMEM(table.shape, F32),
            pltpu.VMEM((AHEAD, rows, LANES), F32),
            pltpu.VMEM((AHEAD, rows, LANES), F32),
            pltpu.SemaphoreType.DMA((4,)),
            pltpu.SemaphoreType.DMA((PARTS,)),
        ],
        in_hbm=range(5),
        flops=rows * samples * 300,
        bytes_accessed=rows * samples * 6,
    )(particles, offsets.T, groups.reshape(1, rows), noise_var.reshape(1, CYCLES), jnp.asarray(table))
    dot_flops = 2 * ROT * classes * rows * samples
    held = [d * owned + o for d in order for o in range(owned)]
    prior = log_prior.reshape(1, classes)
    scored = [((HALF * classes, 2 * rows), F32), ((1, rows), F32), ((1, rows), F32)]
    spots = [pltpu.VMEM((classes * samples // LANES, LANES), F32)]
    wide = [pltpu.VMEM((message, LANES), F32)]
    costs = dict(flops=dot_flops, bytes_accessed=rows * samples * 4)
    summed = [((classes, 2, ACROSS * LANES), BF16)]
    two = cls_size == 2
    e, best, lse = call(functools.partial(first_score_kernel, held, not two), scored, spots, **costs)(
        got, turned, power, prior
    )
    if two:
        early = lax.ppermute(lse, "cls", [(0, 1), (1, 0)])
        e, best, lse = call(functools.partial(second_score_kernel, held), scored, spots, **costs)(
            got, turned, power, prior, e, best, lse
        )
        all_lse = (lse, lax.ppermute(lse, "cls", [(0, 1), (1, 0)]))
        (part,) = call(functools.partial(first_sum_kernel, False), summed, wide, **costs)(
            e, best, adjusted, power, lse, early
        )
        (partial_sums,) = call(second_sum_kernel, summed, wide, **costs)(e, best, adjusted, power, *all_lse, part)
    else:
        all_lse = (lax.all_gather(lse, "cls", axis=0, tiled=True),)
        (partial_sums,) = call(functools.partial(first_sum_kernel, True), summed, wide, **costs)(
            e, best, adjusted, power, *all_lse
        )
    mine = exchange(partial_sums)
    data, weight, evidence = call(
        functools.partial(final_kernel, dom_size),
        [((owned, samples), F32), ((owned, CYCLES), F32), ((1, rows), F32)],
        bytes_accessed=message * LANES * 2,
    )(mine, *all_lse)
    return data, weight, evidence.reshape(rows)


def solution(mesh):
    return jax.shard_map(
        per_device,
        mesh=mesh,
        in_specs=(P("dom", None), P(("cls", "dom"), None), P("cls"), P(), P("dom", None), P("dom")),
        out_specs=(P(("cls", "dom"), None), P(("cls", "dom"), None), P("dom")),
        check_vma=False,
    )
```
